128 devices in a mesh: elem: 32 (over x, y_hi, z), face: 4 (over y_lo, core).
Axes of the slice: x: 4, y: 4 (y_hi: 2, y_lo: 2; y = y_hi * 2 + y_lo), z: 4, core: 2. Of those that a mesh axis runs over, the one named last changes fastest.
Arguments:
- state: bfloat16 [512, 512, 768], P('elem', 'face'), may hold values from -6 to 6
- perturbation: bfloat16 [512, 512, 768], P('elem', 'face'), may hold values from -6 to 6
- adjoint_end: bfloat16 [512, 512, 768], P('elem', 'face'), may hold values from -6 to 6
- kappa: float32 [512, 512], P('elem', 'face'), may hold values from 0.1 to 0.24
- act_list: int32 [32, 4096], P('elem', 'face'), may hold values from 0 to 2047, as said below
- counts: int32 [32, 4], P('elem', 'face'), may hold values from 128 to 1024
- w_in: bfloat16 [768, 512], replicated, may hold values from -0.21875 to 0.21875
- w_mid: bfloat16 [3, 512, 512], replicated, may hold values from -0.25 to 0.25
- w_out: bfloat16 [512, 128], replicated, may hold values from -0.25 to 0.25
- biases: float32 [4, 512], replicated, may hold values from -3 to 3
Outputs:
- tl_out: float32 [512, 512, 768], P('elem', 'face')
- ad_out: float32 [512, 512, 768], P('elem', 'face')
The draws below stay inside these ranges and needn't reach their ends.
Inputs may be any that keep to these rules, and one draw needn't show every extreme that they name: `act_list`: within each tile's 1024 entries the numbers are distinct columns of that tile, numbered row by row over its 16 x 128 columns.
All inputs are finite; a program needn't handle non-finite values.
Results may differ from the reference program's by a relative error of at most 0.0029.
Values may be sent and summed in bfloat16 or wider, within the bound.
No kernel may reach another device: no remote copies, remote signals or barrier semaphores. Data moves between devices by JAX's collectives and lax.ppermute only.
A program may use at most 192 MiB of HBM per device.

```python
import math
import jax
import jax.numpy as jnp
from jax import lax

CX = 16
CY = 128
LEV = 128
D_IN = 768
HID = 512
LAYERS = 4
SUBSTEPS = 3
CAP = 1024
ELEM_TILES = 32
FACE_TILES = 4
NX = 512
NY = 512


def draw_counts(key, part):
    key = jax.random.fold_in(key, 11)
    first, second, third, fourth = jax.random.split(key, 4)
    tiles = ELEM_TILES * FACE_TILES
    base = jax.random.randint(first, (tiles,), CAP // 8, CAP // 3 + 1)
    peaked = jax.random.randint(second, (tiles,), 0, 8) == 0
    chosen = jax.random.randint(third, (), 0, tiles)
    lowest = (chosen + 1 + jax.random.randint(fourth, (), 0, tiles - 1)) % tiles
    places = jnp.arange(tiles)
    values = jnp.where(peaked | (places == chosen), CAP, base)
    values = jnp.where(places == lowest, CAP // 8, values)
    return values.reshape(ELEM_TILES, FACE_TILES).astype(jnp.int32)


def draw_act_list(key, part):
    key = jax.random.fold_in(key, 23)
    keys = jax.random.split(key, ELEM_TILES * FACE_TILES)
    lists = jax.vmap(lambda single: jax.random.permutation(single, CX * CY)[:CAP])(keys)
    return lists.reshape(ELEM_TILES, FACE_TILES * CAP).astype(jnp.int32)


def shard_levels(key, extent, pieces, smallest, largest):
    loudness, own = 1.0, jax.random.fold_in(key, 6)
    for position, shards_of in pieces:
        steps = jnp.exp(jax.random.uniform(jax.random.fold_in(own, position), (shards_of,), jnp.float32, smallest / len(pieces), largest / len(pieces)))
        loudness = loudness * jnp.repeat(steps, extent[position] // shards_of).reshape([-1 if axis == position else 1 for axis in range(len(extent))])
    return loudness


def normal_values(own_key, shape, spread, reach, pieces=(), kind=jnp.bfloat16):
    result = spread * jax.random.normal(own_key, shape, jnp.float32)
    if pieces:
        result = result * shard_levels(own_key, shape, pieces, -0.22, 0.18)
    return jnp.clip(result, -reach, reach).astype(kind)


def setup_inputs(seed: int = 0) -> dict:
    splits = jax.random.split(jax.random.key(seed), 11)
    state = normal_values(splits[0], (NX, NY, D_IN), 1.0, 6.0, ((0, 32), (1, 4)))
    perturbation = normal_values(splits[1], (NX, NY, D_IN), 1.0, 6.0, ((0, 32), (1, 4)))
    adjoint_end = normal_values(splits[2], (NX, NY, D_IN), 1.0, 6.0, ((0, 32), (1, 4)))
    kappa = jnp.clip(jnp.exp(math.log(0.24) - 0.8754687 * jax.random.uniform(splits[3], (NX, NY), jnp.float32) ** shard_levels(splits[3], (NX, NY), ((0, 32), (1, 4)), -0.2, 0.2)), 0.1, 0.24)
    act_list = draw_act_list(jax.random.fold_in(splits[10], 71), 0)
    counts = draw_counts(jax.random.fold_in(splits[10], 71), 0)
    w_in = normal_values(splits[6], (D_IN, HID), D_IN ** -0.5, 0.21875)
    w_mid = normal_values(splits[7], (LAYERS - 1, HID, HID), HID ** -0.5, 0.25)
    w_out = normal_values(splits[8], (HID, LEV), HID ** -0.5, 0.25)
    biases = normal_values(splits[9], (LAYERS, HID), 0.5, 3.0, (), jnp.float32)
    return dict(state=state, perturbation=perturbation, adjoint_end=adjoint_end, kappa=kappa, act_list=act_list, counts=counts, w_in=w_in, w_mid=w_mid, w_out=w_out, biases=biases)


PHYS_STEP = 4.0


def five_point(extended):
    return extended[2:, 1:-1] + extended[:-2, 1:-1] + extended[1:-1, 2:] + extended[1:-1, :-2] - 4.0 * extended[1:-1, 1:-1]


def laplace(field):
    return five_point(jnp.pad(field, ((1, 1), (1, 1), (0, 0))))


def contract_back(left, right):
    return lax.dot_general(left, right, (((1,), (1,)), ((), ())), preferred_element_type=jnp.float32)


def forward_block(x_rows, d_rows, layer_weights, biases, w_out):
    hidden = x_rows
    tangent = d_rows
    slopes = []
    for layer in range(len(layer_weights)):
        preact = jnp.dot(hidden, layer_weights[layer], preferred_element_type=jnp.float32) + biases[layer]
        value = jnp.tanh(preact)
        slope = 1.0 - value * value
        hidden = value.astype(jnp.bfloat16)
        tangent = (slope * jnp.dot(tangent, layer_weights[layer], preferred_element_type=jnp.float32)).astype(jnp.bfloat16)
        slopes.append(slope)
    return jnp.dot(tangent, w_out, preferred_element_type=jnp.float32), jnp.stack(slopes)


def backward_block(upstream_rows, slopes, layer_weights, w_out):
    pulled = contract_back(upstream_rows, w_out)
    for layer in reversed(range(len(layer_weights))):
        scaled = (pulled * slopes[layer]).astype(jnp.bfloat16)
        pulled = contract_back(scaled, layer_weights[layer])
    return pulled


def by_groups(field, update):
    groups = field.shape[2] // LEV
    parts = field.reshape(NX, NY, groups, LEV).transpose(2, 0, 1, 3)
    done = lax.map(update, parts)
    return done.transpose(1, 2, 0, 3).reshape(NX, NY, groups * LEV)


def to_tiles(field):
    width = field.shape[-1]
    return field.reshape(ELEM_TILES, CX, FACE_TILES, CY, width).transpose(0, 2, 1, 3, 4).reshape(ELEM_TILES * FACE_TILES, CX * CY, width)


def from_tiles(tiles):
    width = tiles.shape[-1]
    return tiles.reshape(ELEM_TILES, FACE_TILES, CX, CY, width).transpose(0, 2, 1, 3, 4).reshape(NX, NY, width)


def reference(state, perturbation, adjoint_end, kappa, act_list, counts, w_in, w_mid, w_out, biases):
    layer_weights = [w_in] + [w_mid[index] for index in range(LAYERS - 1)]
    kappa_cells = kappa[:, :, None]

    def adjoint_steps(part):
        for substep in range(SUBSTEPS):
            part = part + laplace(kappa_cells * part)
        return part

    def tangent_steps(part):
        for substep in range(SUBSTEPS):
            part = part + kappa_cells * laplace(part)
        return part

    adjoint = by_groups(adjoint_end.astype(jnp.float32), adjoint_steps)
    state_tiles = to_tiles(state)
    pert_tiles = to_tiles(perturbation)
    adjoint_tiles = to_tiles(adjoint[:, :, :LEV])
    lists = act_list.reshape(ELEM_TILES * FACE_TILES, CAP)
    tile_counts = counts.reshape(ELEM_TILES * FACE_TILES)

    def one_tile(inputs):
        state_cols, pert_cols, adjoint_cols, index, count = inputs
        live = (jnp.arange(CAP, dtype=jnp.int32) < count).astype(jnp.float32)[:, None]
        jac_tl, slopes = forward_block(jnp.take(state_cols, index, axis=0), jnp.take(pert_cols, index, axis=0), layer_weights, biases, w_out)
        upstream = (PHYS_STEP * live * jnp.take(adjoint_cols, index, axis=0)).astype(jnp.bfloat16)
        pulled = backward_block(upstream, slopes, layer_weights, w_out)
        tendency = jnp.zeros((CX * CY, LEV), jnp.float32).at[index].add(PHYS_STEP * live * jac_tl)
        sensitivity = jnp.zeros((CX * CY, D_IN), jnp.float32).at[index].add(pulled)
        return tendency, sensitivity

    tendency, sensitivity = lax.map(one_tile, (state_tiles, pert_tiles, adjoint_tiles, lists, tile_counts))
    tendency = from_tiles(tendency)
    sensitivity = from_tiles(sensitivity)
    moved = perturbation.astype(jnp.float32)
    moved = jnp.concatenate([moved[:, :, :LEV] + tendency, moved[:, :, LEV:]], axis=2)
    tl_out = by_groups(moved, tangent_steps)
    ad_out = adjoint + sensitivity
    return tl_out, ad_out
```

```python
import jax
import jax.numpy as jnp
import numpy as np
from jax import lax
from jax.experimental import pallas as pl
from jax.experimental.pallas import tpu as pltpu
from jax.sharding import PartitionSpec as P

PHYS_STEP = 4.0
REACH = 3
LANES = 128
SIDE = 8
CORNERS = 16
F32 = jnp.float32
BF16 = jnp.bfloat16
VMEM = 60 * 1024 * 1024


def _params(count=1):
    return pltpu.CompilerParams(
        dimension_semantics=("arbitrary",) * count, vmem_limit_bytes=VMEM
    )


def _dot(a, b):
    return jnp.dot(a, b, preferred_element_type=F32)


def _dot_t(a, b):
    return lax.dot_general(a, b, (((1,), (1,)), ((), ())), preferred_element_type=F32)


def _pick(shape, targets):
    row = lax.broadcasted_iota(jnp.int32, shape, 0)
    col = lax.broadcasted_iota(jnp.int32, shape, 1)
    hit = jnp.zeros(shape, jnp.bool_)
    for k, c in targets:
        hit = hit | ((row == k) & (col == c))
    return hit.astype(F32).astype(BF16)


def _split(value):
    hi = value.astype(BF16)
    return hi, (value - hi.astype(F32)).astype(BF16)


def edge_kernel(
    counts, listed, kappa, s_lo, s_hi, p_lo, p_hi, a_lo, a_hi, left, right, mask_out
):
    size_x, size_y = kappa.shape
    width = s_lo.shape[1]
    channels = s_lo.shape[2]
    count = counts[0, 0]
    index = listed[...]
    cap = index.shape[1]
    shift = size_y.bit_length() - 1
    pos = lax.broadcasted_iota(jnp.int32, (size_x, cap), 1)
    sub = lax.broadcasted_iota(jnp.int32, (size_x, cap), 0)
    rows = ((sub == (index >> shift)) & (pos < count)).astype(F32).astype(BF16)
    sub_y = lax.broadcasted_iota(jnp.int32, (size_y, cap), 0)
    cols = (sub_y == (index & (size_y - 1))).astype(F32).astype(BF16)
    mask = _dot_t(rows, cols)
    mask_t = _dot_t(cols, rows)
    for x in range(size_x):
        mask_out[x * size_y : (x + 1) * size_y, :] = jnp.broadcast_to(
            mask_t[:, x : x + 1], (size_y, LANES)
        ).astype(BF16)
    k_all = kappa[...]
    shape = (REACH * size_x, size_x * width)
    row = lax.broadcasted_iota(jnp.int32, shape, 0)
    col = lax.broadcasted_iota(jnp.int32, shape, 1)
    want = (row % size_x) * width + row // size_x
    for msg, blocks, first in (
        (left, (s_lo, p_lo, a_lo), 0),
        (right, (s_hi, p_hi, a_hi), size_y - REACH),
    ):
        pick = (col == want + first % width).astype(F32).astype(BF16)
        for n, block in enumerate(blocks):
            msg[:, n * channels : (n + 1) * channels] = _dot(
                pick, block[...].reshape(size_x * width, channels)
            ).astype(BF16)
        at = len(blocks) * channels
        for j in range(REACH):
            here = slice(j * size_x, (j + 1) * size_x)
            y = first + j
            hi, lo = _split(jnp.broadcast_to(k_all[:, y : y + 1], (size_x, LANES)))
            msg[here, at : at + LANES] = jnp.broadcast_to(
                mask[:, y : y + 1], (size_x, LANES)
            ).astype(BF16)
            msg[here, at + LANES : at + 2 * LANES] = hi
            msg[here, at + 2 * LANES : at + 3 * LANES] = lo


def make_edges(counts, listed, kappa, state, pert, adj):
    size_x, size_y, channels = state.shape
    width = 16
    last = size_y // width - 1
    low = pl.BlockSpec((size_x, width, channels), lambda i: (0, 0, 0))
    high = pl.BlockSpec((size_x, width, channels), lambda i: (0, last, 0))
    strip = jax.ShapeDtypeStruct((REACH * size_x, 3 * channels + 3 * LANES), BF16)
    return pl.pallas_call(
        edge_kernel,
        grid=(1,),
        in_specs=[
            pl.BlockSpec(memory_space=pltpu.SMEM),
            pl.BlockSpec(listed.shape, lambda i: (0, 0)),
            pl.BlockSpec(kappa.shape, lambda i: (0, 0)),
            low, high, low, high, low, high,
        ],
        out_specs=[
            pl.BlockSpec(strip.shape, lambda i: (0, 0)),
            pl.BlockSpec(strip.shape, lambda i: (0, 0)),
            pl.BlockSpec((size_x * size_y, LANES), lambda i: (0, 0)),
        ],
        out_shape=[strip, strip, jax.ShapeDtypeStruct((size_x * size_y, LANES), BF16)],
        compiler_params=_params(),
        name="edges",
    )(counts, listed, kappa, state, state, pert, pert, adj, adj)


def _corner_picks(size_x, top):
    near, next_ = (0, 1) if top else (size_x - 1, size_x - 2)
    left = [(0, 2 * size_x + near), (1, size_x + near), (2, 2 * size_x + next_)]
    right = [(3, near), (4, size_x + near), (5, next_)]
    shape = (CORNERS, REACH * size_x)
    return _pick(shape, left), _pick(shape, right)


def _kappa_wide(kappa, aux_l, aux_r):
    size_x, size_y = kappa.shape
    wide = jnp.concatenate([kappa[...], jnp.zeros((size_x, LANES), F32)], axis=1)
    lane = lax.broadcasted_iota(jnp.int32, wide.shape, 1)
    for aux, first in ((aux_l, wide.shape[1] - REACH), (aux_r, size_y)):
        for j in range(REACH):
            here = slice(j * size_x, (j + 1) * size_x)
            value = aux[here, LANES : 2 * LANES].astype(F32) + aux[
                here, 2 * LANES : 3 * LANES
            ].astype(F32)
            wide = jnp.where(lane == first + j, jnp.concatenate([value, value], axis=1), wide)
    return wide


def adjoint_border_kernel(kappa, aux_l, aux_r, strip_l, strip_r, rows_t, rows_b, top, bot):
    size_x, size_y = kappa.shape
    channels = strip_l.shape[1]
    body = REACH * size_y
    hi, lo = _split(_kappa_wide(kappa, aux_l, aux_r))
    extra = jnp.zeros((size_x, channels - 2 * hi.shape[1]), BF16)
    for msg, rows, is_top in ((top, rows_t, True), (bot, rows_b, False)):
        first = 0 if is_top else rows.shape[0] - REACH
        msg[0:body, :] = rows[first : first + REACH].reshape(body, channels)
        pick_l, pick_r = _corner_picks(size_x, is_top)
        msg[body : body + CORNERS, :] = (
            _dot(pick_l, strip_l[...]) + _dot(pick_r, strip_r[...])
        ).astype(BF16)
        msg[body + CORNERS :, :] = jnp.concatenate([hi, lo, extra], axis=1)


def adjoint_border(kappa, from_l, from_r, adj):
    size_x, size_y, channels = adj.shape
    block = 4
    last = size_x // block - 1
    out = jax.ShapeDtypeStruct((REACH * size_y + CORNERS + size_x, channels), BF16)
    strip = pl.BlockSpec((REACH * size_x, channels), lambda i: (0, 2))
    aux = pl.BlockSpec((REACH * size_x, 3 * LANES), lambda i: (0, channels // LANES))
    return pl.pallas_call(
        adjoint_border_kernel,
        grid=(1,),
        in_specs=[
            pl.BlockSpec(kappa.shape, lambda i: (0, 0)),
            aux, aux, strip, strip,
            pl.BlockSpec((block, size_y, channels), lambda i: (0, 0, 0)),
            pl.BlockSpec((block, size_y, channels), lambda i: (last, 0, 0)),
        ],
        out_specs=[pl.BlockSpec(out.shape, lambda i: (0, 0))] * 2,
        out_shape=[out, out],
        compiler_params=_params(),
        name="adjoint_border",
    )(kappa, from_l, from_r, from_l, from_r, adj, adj)


def tangent_border_kernel(strip_l, strip_r, moved_s, rows_t, rows_b, moved_t, moved_b, top, bot):
    channels = strip_l.shape[1]
    size_y = rows_t.shape[1]
    size_x = strip_l.shape[0] // REACH
    body = REACH * size_y
    for msg, rows, moved, is_top in (
        (top, rows_t, moved_t, True),
        (bot, rows_b, moved_b, False),
    ):
        first = 0 if is_top else rows.shape[0] - REACH
        msg[0:body, :LANES] = moved[first * size_y : (first + REACH) * size_y]
        msg[0:body, LANES:] = rows[first : first + REACH, :, LANES:].reshape(
            body, channels - LANES
        )
        pick_l, pick_r = _corner_picks(size_x, is_top)
        cut = REACH * size_x
        msg[body:, :LANES] = (
            _dot(pick_l, moved_s[:cut]) + _dot(pick_r, moved_s[cut:])
        ).astype(BF16)
        msg[body:, LANES:] = (
            _dot(pick_l, strip_l[:, LANES:]) + _dot(pick_r, strip_r[:, LANES:])
        ).astype(BF16)


def tangent_border(from_l, from_r, moved_strips, pert, moved):
    size_x, size_y, channels = pert.shape
    block = 4
    last = size_x // block - 1
    out = jax.ShapeDtypeStruct((REACH * size_y + CORNERS, channels), BF16)
    strip = pl.BlockSpec((REACH * size_x, channels), lambda i: (0, 1))
    return pl.pallas_call(
        tangent_border_kernel,
        grid=(1,),
        in_specs=[
            strip, strip,
            pl.BlockSpec(moved_strips.shape, lambda i: (0, 0)),
            pl.BlockSpec((block, size_y, channels), lambda i: (0, 0, 0)),
            pl.BlockSpec((block, size_y, channels), lambda i: (last, 0, 0)),
            pl.BlockSpec((block * size_y, LANES), lambda i: (0, 0)),
            pl.BlockSpec((block * size_y, LANES), lambda i: (last, 0)),
        ],
        out_specs=[pl.BlockSpec(out.shape, lambda i: (0, 0))] * 2,
        out_shape=[out, out],
        compiler_params=_params(),
        name="tangent_border",
    )(from_l, from_r, moved_strips, pert, pert, moved, moved)


def _forward(h, t, w_in, w_mid, w_out, biases, slopes):
    rows = h.shape[0]
    units = w_in.shape[1]
    for layer in range(1 + w_mid.shape[0]):
        weights = w_in[...] if layer == 0 else w_mid[layer - 1]
        a = _dot(h, weights) + biases[layer : layer + 1, :]
        v = jnp.tanh(a)
        slope = 1.0 - v * v
        h = v.astype(BF16)
        t = (slope * _dot(t, weights)).astype(BF16)
        if slopes is not None:
            slopes[0:rows, layer * units : (layer + 1) * units] = slope.astype(BF16)
    return _dot(t, w_out[...])


def forward_kernel(
    state, pert, mask, s_l, s_r, p_l, p_r, aux_l, aux_r, w_in, w_mid, w_out, biases,
    slopes, moved, moved_s,
):
    step = pl.program_id(0)
    blocks = pl.num_programs(0) - 1

    @pl.when(step < blocks)
    def _():
        channels = state.shape[2]
        x = state[...].reshape(-1, channels)
        d = pert[...].reshape(-1, channels)
        jac = _forward(x, d, w_in, w_mid, w_out, biases, slopes)
        moved[...] = (
            d[:, :LANES].astype(F32) + PHYS_STEP * mask[...].astype(F32) * jac
        ).astype(BF16)

    @pl.when(step == blocks)
    def _():
        x = jnp.concatenate([s_l[...], s_r[...]], axis=0)
        d = jnp.concatenate([p_l[...], p_r[...]], axis=0)
        live = jnp.concatenate([aux_l[:, :LANES], aux_r[:, :LANES]], axis=0)
        jac = _forward(x, d, w_in, w_mid, w_out, biases, None)
        moved_s[...] = (
            d[:, :LANES].astype(F32) + PHYS_STEP * live.astype(F32) * jac
        ).astype(BF16)


def forward(state, pert, mask, from_l, from_r, w_in, w_mid, w_out, biases):
    size_x, size_y, channels = state.shape
    columns = size_x * size_y
    xs = 2
    rows = xs * size_y
    blocks = size_x // xs
    layers, units = biases.shape
    cut = REACH * size_x
    whole = lambda a: pl.BlockSpec(a.shape, lambda i: (0,) * a.ndim)
    own = lambda i: (jnp.minimum(i, blocks - 1), 0, 0)
    own2 = lambda i: (jnp.minimum(i, blocks - 1), 0)
    strip = lambda n: pl.BlockSpec((cut, channels), lambda i: (0, n))
    aux = pl.BlockSpec((cut, 3 * LANES), lambda i: (0, channels // LANES))
    return pl.pallas_call(
        forward_kernel,
        grid=(blocks + 1,),
        in_specs=[
            pl.BlockSpec((xs, size_y, channels), own),
            pl.BlockSpec((xs, size_y, channels), own),
            pl.BlockSpec((rows, LANES), own2),
            strip(0), strip(0), strip(1), strip(1), aux, aux,
            whole(w_in), whole(w_mid), whole(w_out), whole(biases),
        ],
        out_specs=[
            pl.BlockSpec((rows, layers * units), own2),
            pl.BlockSpec((rows, LANES), own2),
            pl.BlockSpec((2 * cut, LANES), lambda i: (0, 0)),
        ],
        out_shape=[
            jax.ShapeDtypeStruct((columns, layers * units), BF16),
            jax.ShapeDtypeStruct((columns, LANES), BF16),
            jax.ShapeDtypeStruct((2 * cut, LANES), BF16),
        ],
        compiler_params=_params(),
        name="forward",
    )(state, pert, mask, from_l, from_r, from_l, from_r, from_l, from_r, w_in, w_mid, w_out, biases)


def _side_picks(size_x):
    frame = size_x + 2 * REACH
    strips = REACH * size_x
    picks = np.zeros((2, frame * SIDE, LANES), np.float32)
    for x in range(size_x):
        for j in range(REACH):
            picks[0, (x + REACH) * SIDE + SIDE - REACH + j, j * size_x + x] = 1
            picks[1, (x + REACH) * SIDE + j, j * size_x + x] = 1
    for base, step, near in ((strips, -1, REACH - 1), (strips + CORNERS, 1, REACH + size_x)):
        for k, (dx, dy) in enumerate(((0, 0), (0, 1), (1, 0))):
            picks[0, (near + step * dx) * SIDE + SIDE - 1 - dy, base + k] = 1
            picks[1, (near + step * dx) * SIDE + dy, base + 3 + k] = 1
    return jnp.asarray(picks.reshape(2 * frame * SIDE, LANES), BF16)


def _fill(frame, own, above, below, strip_l, strip_r, picks, size_x, size_y):
    row = size_y + 2 * SIDE
    count = size_x + 2 * REACH
    body = REACH * size_y
    half = count * SIDE
    spare = jnp.zeros((LANES - strip_l.shape[0] - 2 * CORNERS, LANES), BF16)
    ends = [above[body : body + CORNERS, :], below[body : body + CORNERS, :], spare]
    side_l = _dot(picks[:half], jnp.concatenate([strip_l] + ends, axis=0))
    side_r = _dot(picks[half:], jnp.concatenate([strip_r] + ends, axis=0))
    for r in range(count):
        at = r * row
        frame[at : at + SIDE, :] = side_l[r * SIDE : (r + 1) * SIDE]
        frame[at + SIDE + size_y : at + row, :] = side_r[r * SIDE : (r + 1) * SIDE]
        if r < REACH:
            value = above[r * size_y : (r + 1) * size_y, :]
        elif r < REACH + size_x:
            value = own[r - REACH]
        else:
            k = r - REACH - size_x
            value = below[k * size_y : (k + 1) * size_y, :]
        frame[at + SIDE : at + SIDE + size_y, :] = value.astype(F32)


def _substep(src, kap, row, r, lo, size):
    at = r * row + lo
    mid = src[at : at + size, :]
    near = (src[at - row : at - row + size, :] + src[at + row : at + row + size, :]) + (
        src[at - 1 : at - 1 + size, :] + src[at + 1 : at + 1 + size, :]
    )
    return mid + kap[at : at + size, :] * (near - 4.0 * mid)


def _transport(ping, pong, kap, size_x, size_y, emit):
    row = size_y + 2 * SIDE
    count = size_x + 2 * REACH
    src, dst = ping, pong
    for step in range(1, REACH):
        for r in range(step, count - step):
            dst[r * row : (r + 1) * row, :] = _substep(src, kap, row, r, 0, row)
        src, dst = dst, src
    for x in range(size_x):
        emit(x, _substep(src, kap, row, x + REACH, SIDE, size_y))


def _kappa_frame(kappa, aux_l, aux_r, above, below, natural, out):
    size_x, size_y = kappa.shape
    row = size_y + 2 * SIDE
    natural[...] = jnp.zeros(natural.shape, F32)
    wide = 2 * LANES
    natural[REACH : REACH + size_x, :] = _kappa_wide(kappa, aux_l, aux_r)
    up = above[:, :wide].astype(F32) + above[:, wide : 2 * wide].astype(F32)
    down = below[:, :wide].astype(F32) + below[:, wide : 2 * wide].astype(F32)
    natural[0:REACH, :] = up[size_x - REACH :]
    natural[REACH + size_x : 2 * REACH + size_x, :] = down[:REACH]
    own = natural[:, :LANES].T
    rest = natural[:, LANES:].T
    for r in range(size_x + 2 * REACH):
        at = r * row
        put = lambda a: jnp.broadcast_to(a[:, r : r + 1], (a.shape[0], LANES))
        out[at : at + SIDE, :] = put(rest[LANES - SIDE :])
        out[at + SIDE : at + SIDE + size_y, :] = put(own)
        out[at + SIDE + size_y : at + row, :] = put(rest[:SIDE])


def adjoint_kernel(
    adj, above, below, strip_l, strip_r, picks, kappa, aux_l, aux_r, k_above, k_below,
    mask, slopes, w_in, w_mid, w_out, kap, out, ping, pong, natural, inverse, moved,
):
    step = pl.program_id(0)
    groups = moved.shape[0]
    size_x, size_y = kappa.shape
    row = size_y + 2 * SIDE

    @pl.when(step == 0)
    def _():
        _kappa_frame(kappa, aux_l, aux_r, k_above, k_below, natural, kap)
        for x in range(size_x):
            at = (x + REACH) * row + SIDE
            inverse[x * size_y : (x + 1) * size_y, :] = 1.0 / kap[at : at + size_y, :]

    @pl.when(step < groups)
    def _():
        _fill(ping, adj, above, below, strip_l[...], strip_r[...], picks, size_x, size_y)
        ping[...] = ping[...] * kap[...]

        def emit(x, value):
            here = slice(x * size_y, (x + 1) * size_y)
            moved[step, here, :] = value * inverse[here, :]

        _transport(ping, pong, kap, size_x, size_y, emit)

    @pl.when(step >= groups)
    def _():
        rows = out.shape[0]
        units = w_in.shape[1]
        here = pl.ds(pl.multiple_of((step - groups) * rows, rows), rows)
        upstream = (PHYS_STEP * mask[...].astype(F32) * moved[0, here, :]).astype(BF16)
        pulled = _dot_t(upstream, w_out[...])
        for layer in reversed(range(1 + w_mid.shape[0])):
            weights = w_in[...] if layer == 0 else w_mid[layer - 1]
            slope = slopes[:, layer * units : (layer + 1) * units].astype(F32)
            pulled = _dot_t((pulled * slope).astype(BF16), weights)
        for g in range(groups):
            lanes = slice(g * LANES, (g + 1) * LANES)
            out[:, lanes] = moved[g, here, :] + pulled[:, lanes]


def adjoint_all(adj, above, below, from_l, from_r, kappa, mask, slopes, w_in, w_mid, w_out):
    size_x, size_y, channels = adj.shape
    columns = size_x * size_y
    groups = channels // LANES
    blocks = 8
    rows = columns // blocks
    row = size_y + 2 * SIDE
    frame = (size_x + 2 * REACH) * row
    cut = REACH * size_x
    picks = _side_picks(size_x)
    ends = REACH * size_y + CORNERS
    whole = lambda a: pl.BlockSpec(a.shape, lambda i: (0,) * a.ndim)
    lane = lambda i: jnp.minimum(i, groups - 1)
    later = lambda i: (jnp.maximum(i - groups, 0), 0)
    border = pl.BlockSpec((ends, LANES), lambda i: (0, lane(i)))
    strip = pl.BlockSpec((cut, LANES), lambda i: (0, 2 * groups + lane(i)))
    aux = pl.BlockSpec((cut, 3 * LANES), lambda i: (0, groups))
    k_rows = pl.BlockSpec((size_x, channels), lambda i: (ends // size_x, 0))
    return pl.pallas_call(
        adjoint_kernel,
        grid=(groups + blocks,),
        in_specs=[
            pl.BlockSpec((size_x, size_y, LANES), lambda i: (0, 0, lane(i))),
            border, border, strip, strip, whole(picks), whole(kappa), aux, aux, k_rows, k_rows,
            pl.BlockSpec((rows, LANES), later),
            pl.BlockSpec((rows, slopes.shape[1]), later),
            whole(w_in), whole(w_mid), whole(w_out),
        ],
        out_specs=[
            pl.BlockSpec((frame, LANES), lambda i: (0, 0)),
            pl.BlockSpec((rows, channels), later),
        ],
        out_shape=[
            jax.ShapeDtypeStruct((frame, LANES), F32),
            jax.ShapeDtypeStruct((columns, channels), F32),
        ],
        scratch_shapes=[
            pltpu.VMEM((frame, LANES), F32),
            pltpu.VMEM((frame, LANES), F32),
            pltpu.VMEM((LANES, 2 * LANES), F32),
            pltpu.VMEM((columns, LANES), F32),
            pltpu.VMEM((groups, columns, LANES), F32),
        ],
        compiler_params=_params(),
        name="adjoint",
    )(adj, above, below, from_l, from_r, picks, kappa, from_l, from_r, above, below,
      mask, slopes, w_in, w_mid, w_out)


def tangent_kernel(
    pert, moved, above, below, strip_l, strip_r, moved_s, picks, kap, out, ping, pong
):
    step = pl.program_id(0)
    size_x, size_y, _ = out.shape
    cut = moved_s.shape[0] // 2

    @pl.when(step == 0)
    def _():
        own = [moved[x * size_y : (x + 1) * size_y, :] for x in range(size_x)]
        _fill(ping, own, above, below, moved_s[:cut], moved_s[cut:], picks, size_x, size_y)

    @pl.when(step > 0)
    def _():
        _fill(ping, pert, above, below, strip_l[...], strip_r[...], picks, size_x, size_y)

    def emit(x, value):
        out[x] = value

    _transport(ping, pong, kap, size_x, size_y, emit)


def tangent_all(pert, moved, moved_strips, above, below, from_l, from_r, kap):
    size_x, size_y, channels = pert.shape
    groups = channels // LANES
    cut = REACH * size_x
    picks = _side_picks(size_x)
    whole = lambda a: pl.BlockSpec(a.shape, lambda i: (0,) * a.ndim)
    border = pl.BlockSpec((above.shape[0], LANES), lambda i: (0, i))
    strip = pl.BlockSpec((cut, LANES), lambda i: (0, groups + i))
    tile = pl.BlockSpec((size_x, size_y, LANES), lambda i: (0, 0, i))
    return pl.pallas_call(
        tangent_kernel,
        grid=(groups,),
        in_specs=[
            tile, whole(moved), border, border, strip, strip, whole(moved_strips),
            whole(picks), whole(kap),
        ],
        out_specs=tile,
        out_shape=jax.ShapeDtypeStruct((size_x, size_y, channels), F32),
        scratch_shapes=[pltpu.VMEM(kap.shape, F32), pltpu.VMEM(kap.shape, F32)],
        compiler_params=_params(),
        name="tangent",
    )(pert, moved, above, below, from_l, from_r, moved_strips, picks, kap)


def _shift(value, axis, way):
    ends = lax.axis_size(axis) - 1
    pairs = [(i, i + 1) if way > 0 else (i + 1, i) for i in range(ends)]
    return lax.ppermute(value, axis, pairs)


def per_device(
    state, perturbation, adjoint_end, kappa, act_list, counts, w_in, w_mid, w_out, biases
):
    size_x, size_y, channels = state.shape
    left, right, mask = make_edges(counts, act_list, kappa, state, perturbation, adjoint_end)
    from_l = _shift(right, "face", 1)
    from_r = _shift(left, "face", -1)
    top, bot = adjoint_border(kappa, from_l, from_r, adjoint_end)
    above = _shift(bot, "elem", 1)
    below = _shift(top, "elem", -1)
    slopes, moved, moved_s = forward(
        state, perturbation, mask, from_l, from_r, w_in, w_mid, w_out, biases
    )
    t_top, t_bot = tangent_border(from_l, from_r, moved_s, perturbation, moved)
    t_above = _shift(t_bot, "elem", 1)
    t_below = _shift(t_top, "elem", -1)
    kap, ad_out = adjoint_all(
        adjoint_end, above, below, from_l, from_r, kappa, mask, slopes, w_in, w_mid, w_out
    )
    tl_out = tangent_all(perturbation, moved, moved_s, t_above, t_below, from_l, from_r, kap)
    return tl_out, ad_out.reshape(size_x, size_y, channels)


def solution(mesh):
    tile = P("elem", "face", None)
    plane = P("elem", "face")
    return jax.shard_map(
        per_device,
        mesh=mesh,
        in_specs=(tile, tile, tile, plane, plane, plane, P(), P(), P(), P()),
        out_specs=(tile, tile),
        check_vma=False,
    )
```

```python
import functools

import jax
import jax.numpy as jnp
import numpy as np
from jax import lax
from jax.experimental import pallas as pl
from jax.experimental.pallas import tpu as pltpu
from jax.sharding import PartitionSpec as P

PHYS_STEP = 4.0
REACH = 3
LANES = 128
SIDE = 8
CORNERS = 16
F32 = jnp.float32
BF16 = jnp.bfloat16
EARLY = 1


def _params(mib):
    return pltpu.CompilerParams(
        dimension_semantics=("arbitrary",), vmem_limit_bytes=mib * 1024 * 1024
    )


def _held():
    return pl.BlockSpec(memory_space=pltpu.VMEM)


def _dot(a, b):
    return jnp.dot(a, b, preferred_element_type=F32)


def _dot_t(a, b):
    return lax.dot_general(a, b, (((1,), (1,)), ((), ())), preferred_element_type=F32)


def _pick(shape, targets):
    row = lax.broadcasted_iota(jnp.int32, shape, 0)
    col = lax.broadcasted_iota(jnp.int32, shape, 1)
    hit = jnp.zeros(shape, jnp.bool_)
    for k, c in targets:
        hit = hit | ((row == k) & (col == c))
    return hit.astype(F32).astype(BF16)


def _split(value):
    hi = value.astype(BF16)
    return hi, (value - hi.astype(F32)).astype(BF16)


def edge_kernel(
    counts, listed_hbm, kappa_hbm, state, pert, adj, left, right, mask_out,
    listed, kappa, near, far, sems,
):
    size_x, size_y = kappa.shape
    width = near.shape[2]
    channels = near.shape[3]
    copies = [
        pltpu.make_async_copy(listed_hbm, listed, sems.at[0]),
        pltpu.make_async_copy(kappa_hbm, kappa, sems.at[1]),
    ]
    for n, field in enumerate((state, pert, adj)):
        low, high = pl.ds(0, width), pl.ds(size_y - width, width)
        copies.append(pltpu.make_async_copy(field.at[:, low], near.at[n], sems.at[2 + 2 * n]))
        copies.append(pltpu.make_async_copy(field.at[:, high], far.at[n], sems.at[3 + 2 * n]))
    for copy in copies:
        copy.start()
    copies[0].wait()
    copies[1].wait()
    count = counts[0, 0]
    index = listed[...]
    cap = index.shape[1]
    shift = size_y.bit_length() - 1
    pos = lax.broadcasted_iota(jnp.int32, (size_x, cap), 1)
    sub = lax.broadcasted_iota(jnp.int32, (size_x, cap), 0)
    rows = ((sub == (index >> shift)) & (pos < count)).astype(F32).astype(BF16)
    sub_y = lax.broadcasted_iota(jnp.int32, (size_y, cap), 0)
    cols = (sub_y == (index & (size_y - 1))).astype(F32).astype(BF16)
    mask = _dot_t(rows, cols)
    mask_t = _dot_t(cols, rows)
    for x in range(size_x):
        mask_out[x * size_y : (x + 1) * size_y, :] = jnp.broadcast_to(
            mask_t[:, x : x + 1], (size_y, LANES)
        ).astype(BF16)
    k_all = kappa[...]
    shape = (REACH * size_x, size_x * width)
    row = lax.broadcasted_iota(jnp.int32, shape, 0)
    col = lax.broadcasted_iota(jnp.int32, shape, 1)
    want = (row % size_x) * width + row // size_x
    for copy in copies[2:]:
        copy.wait()
    for msg, blocks, first in ((left, near, 0), (right, far, size_y - REACH)):
        pick = (col == want + first % width).astype(F32).astype(BF16)
        for n in range(3):
            msg[:, n * channels : (n + 1) * channels] = _dot(
                pick, blocks[n].reshape(size_x * width, channels)
            ).astype(BF16)
        at = 3 * channels
        for j in range(REACH):
            here = slice(j * size_x, (j + 1) * size_x)
            y = first + j
            hi, lo = _split(jnp.broadcast_to(k_all[:, y : y + 1], (size_x, LANES)))
            msg[here, at : at + LANES] = jnp.broadcast_to(
                mask[:, y : y + 1], (size_x, LANES)
            ).astype(BF16)
            msg[here, at + LANES : at + 2 * LANES] = hi
            msg[here, at + 2 * LANES : at + 3 * LANES] = lo


def make_edges(counts, listed, kappa, state, pert, adj):
    size_x, size_y, channels = state.shape
    width = 16
    strip = jax.ShapeDtypeStruct((REACH * size_x, 3 * channels + 3 * LANES), BF16)
    far = pl.BlockSpec(memory_space=pltpu.HBM)
    return pl.pallas_call(
        edge_kernel,
        in_specs=[pl.BlockSpec(memory_space=pltpu.SMEM)] + [far] * 5,
        out_specs=[_held()] * 3,
        out_shape=[strip, strip, jax.ShapeDtypeStruct((size_x * size_y, LANES), BF16)],
        scratch_shapes=[
            pltpu.VMEM(listed.shape, jnp.int32),
            pltpu.VMEM(kappa.shape, F32),
            pltpu.VMEM((3, size_x, width, channels), BF16),
            pltpu.VMEM((3, size_x, width, channels), BF16),
            pltpu.SemaphoreType.DMA((8,)),
        ],
        compiler_params=pltpu.CompilerParams(vmem_limit_bytes=12 * 1024 * 1024),
        name="edges",
    )(counts, *[pltpu.with_memory_space_constraint(a, pltpu.HBM) for a in (listed, kappa, state, pert, adj)])


def _corner_picks(size_x, top):
    near, next_ = (0, 1) if top else (size_x - 1, size_x - 2)
    left = [(0, 2 * size_x + near), (1, size_x + near), (2, 2 * size_x + next_)]
    right = [(3, near), (4, size_x + near), (5, next_)]
    shape = (CORNERS, REACH * size_x)
    return _pick(shape, left), _pick(shape, right)


def _kappa_wide(kappa, aux_l, aux_r):
    size_x, size_y = kappa.shape
    wide = jnp.concatenate([kappa[...], jnp.zeros((size_x, LANES), F32)], axis=1)
    lane = lax.broadcasted_iota(jnp.int32, wide.shape, 1)
    for aux, first in ((aux_l, wide.shape[1] - REACH), (aux_r, size_y)):
        for j in range(REACH):
            here = slice(j * size_x, (j + 1) * size_x)
            value = aux[here, LANES : 2 * LANES].astype(F32) + aux[
                here, 2 * LANES : 3 * LANES
            ].astype(F32)
            wide = jnp.where(lane == first + j, jnp.concatenate([value, value], axis=1), wide)
    return wide


def border_kernel(kappa, from_l, from_r, adj_t, adj_b, pert_t, pert_b, top, bot):
    size_x, size_y = kappa.shape
    channels = adj_t.shape[2]
    body = REACH * size_y
    early = EARLY * LANES
    aux = 3 * channels
    hi, lo = _split(_kappa_wide(kappa, from_l[:, aux:], from_r[:, aux:]))
    extra = jnp.zeros((size_x, channels + early - 2 * hi.shape[1]), BF16)
    for msg, adj, pert, is_top in ((top, adj_t, pert_t, True), (bot, adj_b, pert_b, False)):
        first = 0 if is_top else adj.shape[0] - REACH
        msg[0:body, :channels] = adj[first : first + REACH].reshape(body, channels)
        msg[0:body, channels:] = pert[
            first : first + REACH, :, LANES : LANES + early
        ].reshape(body, early)
        pick_l, pick_r = _corner_picks(size_x, is_top)
        here = slice(body, body + CORNERS)
        msg[here, :channels] = (
            _dot(pick_l, from_l[:, 2 * channels : aux])
            + _dot(pick_r, from_r[:, 2 * channels : aux])
        ).astype(BF16)
        lanes = slice(channels + LANES, channels + LANES + early)
        msg[here, channels:] = (
            _dot(pick_l, from_l[:, lanes]) + _dot(pick_r, from_r[:, lanes])
        ).astype(BF16)
        msg[body + CORNERS :, :] = jnp.concatenate([hi, lo, extra], axis=1)


def first_border(kappa, from_l, from_r, adj, pert):
    size_x, size_y, channels = adj.shape
    block = 4
    last = size_x // block - 1
    whole = lambda a: pl.BlockSpec(a.shape, lambda i: (0,) * a.ndim)
    low = pl.BlockSpec((block, size_y, channels), lambda i: (0, 0, 0))
    high = pl.BlockSpec((block, size_y, channels), lambda i: (last, 0, 0))
    shape = (REACH * size_y + CORNERS + size_x, channels + EARLY * LANES)
    out = jax.ShapeDtypeStruct(shape, BF16)
    return pl.pallas_call(
        border_kernel,
        grid=(1,),
        in_specs=[whole(kappa), whole(from_l), whole(from_r), low, high, low, high],
        out_specs=[whole(out)] * 2,
        out_shape=[out, out],
        compiler_params=_params(12),
        name="first_border",
    )(kappa, from_l, from_r, adj, adj, pert, pert)


def late_border_kernel(from_l, from_r, moved_s, pert_t, pert_b, moved_t, moved_b, top, bot):
    size_y, channels = pert_t.shape[1:]
    size_x = moved_s.shape[0] // (2 * REACH)
    body = REACH * size_y
    cut = REACH * size_x
    lanes = slice((1 + EARLY) * LANES, channels)
    side = slice(channels + lanes.start, 2 * channels)
    for msg, pert, moved, is_top in (
        (top, pert_t, moved_t, True),
        (bot, pert_b, moved_b, False),
    ):
        first = 0 if is_top else pert.shape[0] - REACH
        msg[0:body, :LANES] = moved[first * size_y : (first + REACH) * size_y]
        msg[0:body, LANES:] = pert[first : first + REACH, :, lanes].reshape(
            body, channels - lanes.start
        )
        pick_l, pick_r = _corner_picks(size_x, is_top)
        msg[body:, :LANES] = (
            _dot(pick_l, moved_s[:cut]) + _dot(pick_r, moved_s[cut:])
        ).astype(BF16)
        msg[body:, LANES:] = (_dot(pick_l, from_l[:, side]) + _dot(pick_r, from_r[:, side])).astype(
            BF16
        )


def late_border(from_l, from_r, moved_s, pert, moved_a, moved_b):
    size_x, size_y, channels = pert.shape
    block = 4
    last = size_x // block - 1
    end = moved_b.shape[0] // (block * size_y) - 1
    whole = lambda a: pl.BlockSpec(a.shape, lambda i: (0,) * a.ndim)
    out = jax.ShapeDtypeStruct(
        (REACH * size_y + CORNERS, channels - EARLY * LANES), BF16
    )
    return pl.pallas_call(
        late_border_kernel,
        grid=(1,),
        in_specs=[
            whole(from_l), whole(from_r), whole(moved_s),
            pl.BlockSpec((block, size_y, channels), lambda i: (0, 0, 0)),
            pl.BlockSpec((block, size_y, channels), lambda i: (last, 0, 0)),
            pl.BlockSpec((block * size_y, LANES), lambda i: (0, 0)),
            pl.BlockSpec((block * size_y, LANES), lambda i: (end, 0)),
        ],
        out_specs=[whole(out)] * 2,
        out_shape=[out, out],
        compiler_params=_params(12),
        name="late_border",
    )(from_l, from_r, moved_s, pert, pert, moved_a, moved_b)


def _forward(pairs, w_in, w_mid, w_out, biases, keep):
    pairs = list(pairs)
    for layer in range(1 + w_mid.shape[0]):
        weights = w_in[...] if layer == 0 else w_mid[layer - 1]
        bias = biases[layer : layer + 1, :]
        for n, (h, t) in enumerate(pairs):
            rows = h.shape[0]
            both = _dot(jnp.concatenate([h, t], axis=0), weights)
            v = jnp.tanh(both[:rows] + bias)
            slope = 1.0 - v * v
            pairs[n] = (v.astype(BF16), (slope * both[rows:]).astype(BF16))
            keep(n, layer, slope)
    return [_dot(t, w_out[...]) for _, t in pairs]


def forward_kernel(first, strips, rows, chunks, *refs):
    if strips:
        (state, pert, mask, from_l, from_r, w_in, w_mid, w_out, biases,
         slopes, moved, moved_s, side_x, side_d, side_m) = refs
    else:
        state, pert, mask, w_in, w_mid, w_out, biases, slopes, moved = refs
    step = pl.program_id(0)
    _, size_y, channels = state.shape
    units = biases.shape[1]
    xs = rows // size_y
    if strips:
        cut = from_l.shape[0]
        each = 2 * cut // pl.num_programs(0)

        @pl.when(step == 0)
        def _():
            for n, msg in enumerate((from_l, from_r)):
                here = slice(n * cut, (n + 1) * cut)
                side_x[here, :] = msg[:, :channels]
                side_d[here, :] = msg[:, channels : 2 * channels]
                side_m[here, :] = msg[:, 3 * channels : 3 * channels + LANES]

        beside = pl.ds(pl.multiple_of(step * each, each), each)
    x_here = pl.ds(first + step * xs, xs)
    x = state[x_here].reshape(rows, channels)
    d = pert[x_here].reshape(rows, channels)
    part = rows // chunks
    pairs = [(x[n * part : (n + 1) * part], d[n * part : (n + 1) * part]) for n in range(chunks)]
    if strips:
        h, t = pairs[-1]
        pairs[-1] = (
            jnp.concatenate([h, side_x[beside, :]], axis=0),
            jnp.concatenate([t, side_d[beside, :]], axis=0),
        )

    def at(n):
        return pl.ds(pl.multiple_of(step * rows + n * part, part), part)

    def keep(n, layer, slope):
        slopes[at(n), layer * units : (layer + 1) * units] = slope[:part].astype(BF16)

    jac = _forward(pairs, w_in, w_mid, w_out, biases, keep)

    def shift(live, value, base):
        return (base.astype(F32) + PHYS_STEP * live.astype(F32) * value).astype(BF16)

    for n in range(chunks):
        here = pl.ds(pl.multiple_of((first + step * xs) * size_y + n * part, part), part)
        base = d[n * part : (n + 1) * part, :LANES]
        moved[at(n), :] = shift(mask[here, :], jac[n][:part], base)
    if strips:
        moved_s[beside, :] = shift(side_m[beside, :], jac[-1][part:], side_d[beside, :LANES])


def forward(first, count, state, pert, mask, sides, weights):
    _, size_y, channels = state.shape
    xs = 4
    rows = xs * size_y
    layers, units = weights[3].shape
    columns = count * size_y
    args = (state, pert, mask) + sides + weights
    out = [
        jax.ShapeDtypeStruct((columns, layers * units), BF16),
        jax.ShapeDtypeStruct((columns, LANES), BF16),
    ]
    scratch = []
    if sides:
        beside = 2 * sides[0].shape[0]
        out.append(jax.ShapeDtypeStruct((beside, LANES), BF16))
        scratch = [
            pltpu.VMEM((beside, channels), BF16),
            pltpu.VMEM((beside, channels), BF16),
            pltpu.VMEM((beside, LANES), BF16),
        ]
    return pl.pallas_call(
        functools.partial(forward_kernel, first, bool(sides), rows, 2),
        grid=(count // xs,),
        in_specs=[_held()] * len(args),
        out_specs=[_held()] * len(out),
        out_shape=out,
        scratch_shapes=scratch,
        compiler_params=_params(14),
        name="forward_rest" if sides else "forward_part",
    )(*args)


def _side_picks(size_x):
    frame = size_x + 2 * REACH
    strips = REACH * size_x
    picks = np.zeros((2, frame * SIDE, LANES), np.float32)
    for x in range(size_x):
        for j in range(REACH):
            picks[0, (x + REACH) * SIDE + SIDE - REACH + j, j * size_x + x] = 1
            picks[1, (x + REACH) * SIDE + j, j * size_x + x] = 1
    for base, step, near in ((strips, -1, REACH - 1), (strips + CORNERS, 1, REACH + size_x)):
        for k, (dx, dy) in enumerate(((0, 0), (0, 1), (1, 0))):
            picks[0, (near + step * dx) * SIDE + SIDE - 1 - dy, base + k] = 1
            picks[1, (near + step * dx) * SIDE + dy, base + 3 + k] = 1
    return jnp.asarray(picks.reshape(2 * frame * SIDE, LANES), BF16)


def _place_sides(out, picks, strip_l, strip_r, ends):
    half = out.shape[0] // 2
    spare = LANES - strip_l.shape[0] - sum(e.shape[0] for e in ends)
    ends = list(ends) + [jnp.zeros((spare, out.shape[1]), BF16)]
    out[:half, :] = _dot(picks[:half, :], jnp.concatenate([strip_l] + ends, axis=0))
    out[half:, :] = _dot(picks[half:, :], jnp.concatenate([strip_r] + ends, axis=0))


def _fill(frame, own, above, below, sides, lanes, size_x, size_y, scale=None):
    row = size_y + 2 * SIDE
    count = size_x + 2 * REACH
    half = count * SIDE

    def put(at, value):
        here = slice(at, at + value.shape[0])
        frame[here, :] = value if scale is None else value * scale[here, :]

    for r in range(count):
        at = r * row
        put(at, sides[r * SIDE : (r + 1) * SIDE, lanes])
        put(at + SIDE + size_y, sides[half + r * SIDE : half + (r + 1) * SIDE, lanes])
        if r < REACH:
            value = above(slice(r * size_y, (r + 1) * size_y))
        elif r < REACH + size_x:
            value = own(r - REACH)
        else:
            k = r - REACH - size_x
            value = below(slice(k * size_y, (k + 1) * size_y))
        put(at + SIDE, value.astype(F32))


def _transport(ping, pong, kap, size_x, size_y, emit):
    row = size_y + 2 * SIDE
    count = size_x + 2 * REACH
    src, dst = ping, pong
    for step in range(1, REACH + 1):
        last = step == REACH
        start, stop = (SIDE, SIDE + size_y) if last else (0, row)
        size = (stop - start) // 2
        for lo in range(start, stop, size):
            at = step * row + lo
            prev = src[at - row : at - row + size, :]
            mid = src[at : at + size, :]
            for r in range(step, count - step):
                at = r * row + lo
                following = src[at + row : at + row + size, :]
                near = (prev + following) + (
                    src[at - 1 : at - 1 + size, :] + src[at + 1 : at + 1 + size, :]
                )
                value = mid + kap[at : at + size, :] * (near - 4.0 * mid)
                if last:
                    emit(r - REACH, lo - SIDE, size, value)
                else:
                    dst[at : at + size, :] = value
                prev, mid = mid, following
        src, dst = dst, src


def _kappa_frame(kappa, aux_l, aux_r, above, below, natural, out):
    size_x, size_y = kappa.shape
    row = size_y + 2 * SIDE
    natural[...] = jnp.zeros(natural.shape, F32)
    wide = 2 * LANES
    natural[REACH : REACH + size_x, :] = _kappa_wide(kappa, aux_l, aux_r)
    up = above[:, :wide].astype(F32) + above[:, wide : 2 * wide].astype(F32)
    down = below[:, :wide].astype(F32) + below[:, wide : 2 * wide].astype(F32)
    natural[0:REACH, :] = up[size_x - REACH :]
    natural[REACH + size_x : 2 * REACH + size_x, :] = down[:REACH]
    own = natural[:, :LANES].T
    rest = natural[:, LANES:].T
    for r in range(size_x + 2 * REACH):
        at = r * row
        put = lambda a: jnp.broadcast_to(a[:, r : r + 1], (a.shape[0], LANES))
        out[at : at + SIDE, :] = put(rest[LANES - SIDE :])
        out[at + SIDE : at + SIDE + size_y, :] = put(own)
        out[at + SIDE + size_y : at + row, :] = put(rest[:SIDE])


def _lanes(group):
    return pl.ds(pl.multiple_of(group * LANES, LANES), LANES)


def adjoint_kernel(
    adj, above, below, from_l, from_r, picks, kappa, mask, slopes_a, slopes_b, w_in, w_mid, w_out,
    kap, out, ping, pong, natural, inverse, moved, sides,
):
    step = pl.program_id(0)
    groups = moved.shape[0]
    size_x, size_y = kappa.shape
    channels = adj.shape[2]
    row = size_y + 2 * SIDE
    body = REACH * size_y
    aux = 3 * channels

    @pl.when(step == 0)
    def _():
        k_rows = slice(body + CORNERS, body + CORNERS + size_x)
        _kappa_frame(
            kappa, from_l[:, aux:], from_r[:, aux:], above[k_rows, :], below[k_rows, :], natural, kap
        )
        for x in range(size_x):
            at = (x + REACH) * row + SIDE
            inverse[x * size_y : (x + 1) * size_y, :] = 1.0 / kap[at : at + size_y, :]
        ends = [m[body : body + CORNERS, :channels] for m in (above, below)]
        strip = slice(2 * channels, aux)
        _place_sides(sides, picks, from_l[:, strip], from_r[:, strip], ends)

    @pl.when(step < groups)
    def _():
        lanes = _lanes(step)
        _fill(
            ping, lambda x: adj[x, :, lanes], lambda r: above[r, lanes], lambda r: below[r, lanes],
            sides, lanes, size_x, size_y, kap,
        )

        def emit(x, lo, size, value):
            here = slice(x * size_y + lo, x * size_y + lo + size)
            moved[step, here, :] = value * inverse[here, :]

        _transport(ping, pong, kap, size_x, size_y, emit)

    rows = out.shape[0]
    units = w_in.shape[1]

    def back(slopes, block, base):
        here = pl.ds(pl.multiple_of(block * rows, rows), rows)
        kept = pl.ds(pl.multiple_of((block - base) * rows, rows), rows)
        upstream = (PHYS_STEP * mask[here, :].astype(F32) * moved[0, here, :]).astype(BF16)
        half = rows // 2
        parts = [_dot_t(upstream[n * half : (n + 1) * half], w_out[...]) for n in range(2)]
        for layer in reversed(range(1 + w_mid.shape[0])):
            weights = w_in[...] if layer == 0 else w_mid[layer - 1]
            slope = slopes[kept, layer * units : (layer + 1) * units]
            for n in range(2):
                part = slope[n * half : (n + 1) * half].astype(F32)
                parts[n] = _dot_t((parts[n] * part).astype(BF16), weights)
        for n in range(2):
            at = pl.ds(pl.multiple_of(block * rows + n * half, half), half)
            for g in range(groups):
                lanes = slice(g * LANES, (g + 1) * LANES)
                out[n * half : (n + 1) * half, lanes] = moved[g, at, :] + parts[n][:, lanes]

    split = slopes_a.shape[0] // rows

    @pl.when((step >= groups) & (step < groups + split))
    def _():
        back(slopes_a, step - groups, 0)

    @pl.when(step >= groups + split)
    def _():
        back(slopes_b, step - groups, split)


def adjoint_all(adj, above, below, from_l, from_r, kappa, mask, slopes_a, slopes_b, weights):
    size_x, size_y, channels = adj.shape
    columns = size_x * size_y
    groups = channels // LANES
    blocks = 4
    rows = columns // blocks
    frame = (size_x + 2 * REACH) * (size_y + 2 * SIDE)
    picks = _side_picks(size_x)
    args = (adj, above, below, from_l, from_r, picks, kappa, mask, slopes_a, slopes_b) + weights
    return pl.pallas_call(
        adjoint_kernel,
        grid=(groups + blocks,),
        in_specs=[_held()] * len(args),
        out_specs=[
            _held(),
            pl.BlockSpec((rows, channels), lambda i: (jnp.maximum(i - groups, 0), 0)),
        ],
        out_shape=[
            jax.ShapeDtypeStruct((frame, LANES), F32),
            jax.ShapeDtypeStruct((columns, channels), F32),
        ],
        scratch_shapes=[
            pltpu.VMEM((frame, LANES), F32),
            pltpu.VMEM((frame, LANES), F32),
            pltpu.VMEM((LANES, 2 * LANES), F32),
            pltpu.VMEM((columns, LANES), F32),
            pltpu.VMEM((groups, columns, LANES), F32),
            pltpu.VMEM((picks.shape[0], channels), F32),
        ],
        compiler_params=_params(26),
        name="adjoint",
    )(*args)


def tangent_kernel(
    pert, moved_a, moved_b, first_t, first_b, late_t, late_b, from_l, from_r, moved_s, picks, kap,
    out, ping, pong, sides,
):
    step = pl.program_id(0)
    size_x, size_y, _ = out.shape
    channels = pert.shape[2]
    cut = moved_s.shape[0] // 2
    body = REACH * size_y
    early = EARLY * LANES

    @pl.when(step == 0)
    def _():
        ends = [
            jnp.concatenate(
                [
                    late[body : body + CORNERS, :LANES],
                    first[body : body + CORNERS, channels : channels + early],
                    late[body : body + CORNERS, LANES:],
                ],
                axis=1,
            )
            for first, late in ((first_t, late_t), (first_b, late_b))
        ]
        strips = [
            jnp.concatenate(
                [moved_s[n * cut : (n + 1) * cut, :], msg[:, channels + LANES : 2 * channels]], axis=1
            )
            for n, msg in enumerate((from_l, from_r))
        ]
        _place_sides(sides, picks, strips[0], strips[1], ends)
        split = moved_a.shape[0] // size_y

        def own(x):
            source, k = (moved_a, x) if x < split else (moved_b, x - split)
            return source[k * size_y : (k + 1) * size_y, :]

        _fill(
            ping, own, lambda r: late_t[r, :LANES], lambda r: late_b[r, :LANES],
            sides, slice(0, LANES), size_x, size_y,
        )

    def fill(top, bot, lanes):
        here = _lanes(step)
        _fill(
            ping, lambda x: pert[x, :, here], lambda r: top[r, lanes], lambda r: bot[r, lanes],
            sides, here, size_x, size_y,
        )

    @pl.when((step > 0) & (step <= EARLY))
    def _():
        fill(first_t, first_b, _lanes(channels // LANES + step - 1))

    @pl.when(step > EARLY)
    def _():
        fill(late_t, late_b, _lanes(step - EARLY))

    def emit(x, lo, size, value):
        out[x, lo : lo + size, :] = value

    _transport(ping, pong, kap, size_x, size_y, emit)


def tangent_all(pert, moved_a, moved_b, first, late, from_l, from_r, moved_s, kap):
    size_x, size_y, channels = pert.shape
    picks = _side_picks(size_x)
    args = (pert, moved_a, moved_b) + first + late + (from_l, from_r, moved_s, picks, kap)
    return pl.pallas_call(
        tangent_kernel,
        grid=(channels // LANES,),
        in_specs=[_held()] * len(args),
        out_specs=pl.BlockSpec((size_x, size_y, LANES), lambda i: (0, 0, i)),
        out_shape=jax.ShapeDtypeStruct((size_x, size_y, channels), F32),
        scratch_shapes=[
            pltpu.VMEM(kap.shape, F32),
            pltpu.VMEM(kap.shape, F32),
            pltpu.VMEM((picks.shape[0], channels), F32),
        ],
        compiler_params=_params(12),
        name="tangent",
    )(*args)


def _shift(value, axis, way):
    ends = lax.axis_size(axis) - 1
    pairs = [(i, i + 1) if way > 0 else (i + 1, i) for i in range(ends)]
    return lax.ppermute(value, axis, pairs)


def per_device(
    state, perturbation, adjoint_end, kappa, act_list, counts, w_in, w_mid, w_out, biases
):
    size_x, size_y, channels = state.shape
    weights = (w_in, w_mid, w_out)
    nets = weights + (biases,)
    part = 4
    left, right, mask = make_edges(counts, act_list, kappa, state, perturbation, adjoint_end)
    from_l = _shift(right, "face", 1)
    from_r = _shift(left, "face", -1)
    slopes_a, moved_a = forward(0, part, state, perturbation, mask, (), nets)
    from_l, from_r, slopes_a = lax.optimization_barrier((from_l, from_r, slopes_a))
    top, bot = first_border(kappa, from_l, from_r, adjoint_end, perturbation)
    first = (_shift(bot, "elem", 1), _shift(top, "elem", -1))
    slopes_b, moved_b, moved_s = forward(
        part, size_x - part, state, perturbation, mask, (from_l, from_r), nets
    )
    top, bot = late_border(from_l, from_r, moved_s, perturbation, moved_a, moved_b)
    late = (_shift(bot, "elem", 1), _shift(top, "elem", -1))
    kap, ad_out = adjoint_all(
        adjoint_end, first[0], first[1], from_l, from_r, kappa, mask, slopes_a, slopes_b, weights
    )
    tl_out = tangent_all(perturbation, moved_a, moved_b, first, late, from_l, from_r, moved_s, kap)
    return tl_out, ad_out.reshape(size_x, size_y, channels)


def solution(mesh):
    tile = P("elem", "face", None)
    plane = P("elem", "face")
    return jax.shard_map(
        per_device,
        mesh=mesh,
        in_specs=(tile, tile, tile, plane, plane, plane, P(), P(), P(), P()),
        out_specs=(tile, tile),
        check_vma=False,
    )
```

```python
import functools

import jax
import jax.numpy as jnp
import numpy as np
from jax import lax
from jax.experimental import pallas as pl
from jax.experimental.pallas import tpu as pltpu
from jax.sharding import PartitionSpec as P

PHYS_STEP = 4.0
REACH = 3
LANES = 128
SIDE = 8
CORNERS = 16
F32 = jnp.float32
BF16 = jnp.bfloat16


def _params(mib):
    return pltpu.CompilerParams(
        dimension_semantics=("arbitrary",), vmem_limit_bytes=mib * 1024 * 1024
    )


def _held():
    return pl.BlockSpec(memory_space=pltpu.VMEM)


def _even(axis):
    return lax.axis_index(axis) % 2 == 0


def _both_ways(axis, act):
    even = _even(axis)

    @pl.when(even)
    def _():
        act(False)

    @pl.when(jnp.logical_not(even))
    def _():
        act(True)


def _dot(a, b):
    return jnp.dot(a, b, preferred_element_type=F32)


def _dot_t(a, b):
    return lax.dot_general(a, b, (((1,), (1,)), ((), ())), preferred_element_type=F32)


def _pick(shape, targets):
    row = lax.broadcasted_iota(jnp.int32, shape, 0)
    col = lax.broadcasted_iota(jnp.int32, shape, 1)
    hit = jnp.zeros(shape, jnp.bool_)
    for k, c in targets:
        hit = hit | ((row == k) & (col == c))
    return hit.astype(F32).astype(BF16)


def _split(value):
    hi = value.astype(BF16)
    return hi, (value - hi.astype(F32)).astype(BF16)


def edge_kernel(
    counts, listed_hbm, kappa_hbm, state, pert, adj, msg_1, msg_2, mask_out,
    listed, kappa, near, far, sems,
):
    size_x, size_y = kappa.shape
    width = near.shape[2]
    channels = near.shape[3]
    copies = [
        pltpu.make_async_copy(listed_hbm, listed, sems.at[0]),
        pltpu.make_async_copy(kappa_hbm, kappa, sems.at[1]),
    ]
    for n, field in enumerate((state, pert, adj)):
        low, high = pl.ds(0, width), pl.ds(size_y - width, width)
        copies.append(pltpu.make_async_copy(field.at[:, low], near.at[n], sems.at[2 + 2 * n]))
        copies.append(pltpu.make_async_copy(field.at[:, high], far.at[n], sems.at[3 + 2 * n]))
    for copy in copies:
        copy.start()
    copies[0].wait()
    copies[1].wait()
    count = counts[0, 0]
    index = listed[...]
    cap = index.shape[1]
    shift = size_y.bit_length() - 1
    pos = lax.broadcasted_iota(jnp.int32, (size_x, cap), 1)
    sub = lax.broadcasted_iota(jnp.int32, (size_x, cap), 0)
    rows = ((sub == (index >> shift)) & (pos < count)).astype(F32).astype(BF16)
    sub_y = lax.broadcasted_iota(jnp.int32, (size_y, cap), 0)
    cols = (sub_y == (index & (size_y - 1))).astype(F32).astype(BF16)
    mask = _dot_t(rows, cols)
    mask_t = _dot_t(cols, rows)
    for x in range(size_x):
        mask_out[x * size_y : (x + 1) * size_y, :] = jnp.broadcast_to(
            mask_t[:, x : x + 1], (size_y, LANES)
        ).astype(BF16)
    k_all = kappa[...]
    shape = (REACH * size_x, size_x * width)
    row = lax.broadcasted_iota(jnp.int32, shape, 0)
    col = lax.broadcasted_iota(jnp.int32, shape, 1)
    want = (row % size_x) * width + row // size_x
    for copy in copies[2:]:
        copy.wait()
    def write(left, right):
        for msg, blocks, first in ((left, near, 0), (right, far, size_y - REACH)):
            pick = (col == want + first % width).astype(F32).astype(BF16)
            for n in range(3):
                msg[:, n * channels : (n + 1) * channels] = _dot(
                    pick, blocks[n].reshape(size_x * width, channels)
                ).astype(BF16)
            at = 3 * channels
            for j in range(REACH):
                here = slice(j * size_x, (j + 1) * size_x)
                y = first + j
                hi, lo = _split(jnp.broadcast_to(k_all[:, y : y + 1], (size_x, LANES)))
                msg[here, at : at + LANES] = jnp.broadcast_to(
                    mask[:, y : y + 1], (size_x, LANES)
                ).astype(BF16)
                msg[here, at + LANES : at + 2 * LANES] = hi
                msg[here, at + 2 * LANES : at + 3 * LANES] = lo

    _both_ways("face", lambda odd: write(msg_1, msg_2) if odd else write(msg_2, msg_1))


def make_edges(counts, listed, kappa, state, pert, adj):
    size_x, size_y, channels = state.shape
    width = 16
    strip = jax.ShapeDtypeStruct((REACH * size_x, 3 * channels + 3 * LANES), BF16)
    far = pl.BlockSpec(memory_space=pltpu.HBM)
    return pl.pallas_call(
        edge_kernel,
        in_specs=[pl.BlockSpec(memory_space=pltpu.SMEM)] + [far] * 5,
        out_specs=[_held()] * 3,
        out_shape=[strip, strip, jax.ShapeDtypeStruct((size_x * size_y, LANES), BF16)],
        scratch_shapes=[
            pltpu.VMEM(listed.shape, jnp.int32),
            pltpu.VMEM(kappa.shape, F32),
            pltpu.VMEM((3, size_x, width, channels), BF16),
            pltpu.VMEM((3, size_x, width, channels), BF16),
            pltpu.SemaphoreType.DMA((8,)),
        ],
        compiler_params=pltpu.CompilerParams(vmem_limit_bytes=12 * 1024 * 1024),
        name="edges",
    )(counts, *[pltpu.with_memory_space_constraint(a, pltpu.HBM) for a in (listed, kappa, state, pert, adj)])


def _corner_picks(size_x, top):
    near, next_ = (0, 1) if top else (size_x - 1, size_x - 2)
    left = [(0, 2 * size_x + near), (1, size_x + near), (2, 2 * size_x + next_)]
    right = [(3, near), (4, size_x + near), (5, next_)]
    shape = (CORNERS, REACH * size_x)
    return _pick(shape, left), _pick(shape, right)


def _kappa_wide(kappa, aux_l, aux_r):
    size_x, size_y = kappa.shape
    wide = jnp.concatenate([kappa[...], jnp.zeros((size_x, LANES), F32)], axis=1)
    lane = lax.broadcasted_iota(jnp.int32, wide.shape, 1)
    for aux, first in ((aux_l, wide.shape[1] - REACH), (aux_r, size_y)):
        for j in range(REACH):
            here = slice(j * size_x, (j + 1) * size_x)
            value = aux[here, LANES : 2 * LANES].astype(F32) + aux[
                here, 2 * LANES : 3 * LANES
            ].astype(F32)
            wide = jnp.where(lane == first + j, jnp.concatenate([value, value], axis=1), wide)
    return wide


def border_kernel(kappa, got_1, got_2, adj_t, adj_b, msg_1, msg_2, strips):
    def order(odd):
        strips[0], strips[1] = (got_1[...], got_2[...]) if odd else (got_2[...], got_1[...])

    _both_ways("face", order)

    def write(odd):
        top, bot = (msg_1, msg_2) if odd else (msg_2, msg_1)
        _write_border(kappa, strips.at[0], strips.at[1], adj_t, adj_b, top, bot)

    _both_ways("elem", write)


def _write_border(kappa, from_l, from_r, adj_t, adj_b, top, bot):
    size_x, size_y = kappa.shape
    channels = adj_t.shape[2]
    body = REACH * size_y
    aux = 3 * channels
    hi, lo = _split(_kappa_wide(kappa, from_l[:, aux:], from_r[:, aux:]))
    extra = jnp.zeros((size_x, channels - 2 * hi.shape[1]), BF16)
    for msg, adj, is_top in ((top, adj_t, True), (bot, adj_b, False)):
        first = 0 if is_top else adj.shape[0] - REACH
        msg[0:body, :] = adj[first : first + REACH].reshape(body, channels)
        pick_l, pick_r = _corner_picks(size_x, is_top)
        here = slice(body, body + CORNERS)
        msg[here, :] = (
            _dot(pick_l, from_l[:, 2 * channels : aux])
            + _dot(pick_r, from_r[:, 2 * channels : aux])
        ).astype(BF16)
        msg[body + CORNERS :, :] = jnp.concatenate([hi, lo, extra], axis=1)


def first_border(kappa, got, adj):
    size_x, size_y, channels = adj.shape
    block = 4
    last = size_x // block - 1
    whole = lambda a: pl.BlockSpec(a.shape, lambda i: (0,) * a.ndim)
    low = pl.BlockSpec((block, size_y, channels), lambda i: (0, 0, 0))
    high = pl.BlockSpec((block, size_y, channels), lambda i: (last, 0, 0))
    shape = (REACH * size_y + CORNERS + size_x, channels)
    out = jax.ShapeDtypeStruct(shape, BF16)
    strips = jax.ShapeDtypeStruct((2,) + got[0].shape, BF16)
    return pl.pallas_call(
        border_kernel,
        grid=(1,),
        in_specs=[whole(kappa), whole(got[0]), whole(got[1]), low, high],
        out_specs=[whole(out), whole(out), whole(strips)],
        out_shape=[out, out, strips],
        compiler_params=_params(12),
        name="first_border",
    )(kappa, got[0], got[1], adj, adj)


def late_border_kernel(strips, moved_s, pert_t, pert_b, moved_t, moved_b, msg_1, msg_2):
    def write(odd):
        top, bot = (msg_1, msg_2) if odd else (msg_2, msg_1)
        _write_late(
            strips.at[0], strips.at[1], moved_s, pert_t, pert_b, moved_t, moved_b, top, bot
        )

    _both_ways("elem", write)


def _write_late(from_l, from_r, moved_s, pert_t, pert_b, moved_t, moved_b, top, bot):
    size_y, channels = pert_t.shape[1:]
    size_x = moved_s.shape[0] // (2 * REACH)
    body = REACH * size_y
    cut = REACH * size_x
    lanes = slice(LANES, channels)
    side = slice(channels + lanes.start, 2 * channels)
    for msg, pert, moved, is_top in (
        (top, pert_t, moved_t, True),
        (bot, pert_b, moved_b, False),
    ):
        first = 0 if is_top else pert.shape[0] - REACH
        msg[0:body, :LANES] = moved[first * size_y : (first + REACH) * size_y]
        msg[0:body, LANES:] = pert[first : first + REACH, :, lanes].reshape(
            body, channels - lanes.start
        )
        pick_l, pick_r = _corner_picks(size_x, is_top)
        msg[body:, :LANES] = (
            _dot(pick_l, moved_s[:cut]) + _dot(pick_r, moved_s[cut:])
        ).astype(BF16)
        msg[body:, LANES:] = (_dot(pick_l, from_l[:, side]) + _dot(pick_r, from_r[:, side])).astype(
            BF16
        )


def late_border(strips, moved_s, pert, moved_a, moved_b):
    size_x, size_y, channels = pert.shape
    block = 4
    last = size_x // block - 1
    end = moved_b.shape[0] // (block * size_y) - 1
    whole = lambda a: pl.BlockSpec(a.shape, lambda i: (0,) * a.ndim)
    out = jax.ShapeDtypeStruct(
        (REACH * size_y + CORNERS, channels), BF16
    )
    return pl.pallas_call(
        late_border_kernel,
        grid=(1,),
        in_specs=[
            whole(strips), whole(moved_s),
            pl.BlockSpec((block, size_y, channels), lambda i: (0, 0, 0)),
            pl.BlockSpec((block, size_y, channels), lambda i: (last, 0, 0)),
            pl.BlockSpec((block * size_y, LANES), lambda i: (0, 0)),
            pl.BlockSpec((block * size_y, LANES), lambda i: (end, 0)),
        ],
        out_specs=[whole(out)] * 2,
        out_shape=[out, out],
        compiler_params=_params(12),
        name="late_border",
    )(strips, moved_s, pert, pert, moved_a, moved_b)


def _forward(pairs, w_in, w_mid, w_out, biases, keep):
    pairs = list(pairs)
    for layer in range(1 + w_mid.shape[0]):
        weights = w_in[...] if layer == 0 else w_mid[layer - 1]
        bias = biases[layer : layer + 1, :]
        for n, (h, t) in enumerate(pairs):
            rows = h.shape[0]
            both = _dot(jnp.concatenate([h, t], axis=0), weights)
            v = jnp.tanh(both[:rows] + bias)
            slope = 1.0 - v * v
            pairs[n] = (v.astype(BF16), (slope * both[rows:]).astype(BF16))
            keep(n, layer, slope)
    return [_dot(t, w_out[...]) for _, t in pairs]


def forward_kernel(first, strips, rows, chunks, *refs):
    if strips:
        (state, pert, mask, beside_all, w_in, w_mid, w_out, biases,
         slopes, moved, moved_s, side_x, side_d, side_m) = refs
    else:
        state, pert, mask, w_in, w_mid, w_out, biases, slopes, moved = refs
    step = pl.program_id(0)
    _, size_y, channels = state.shape
    units = biases.shape[1]
    xs = rows // size_y
    if strips:
        cut = beside_all.shape[1]
        each = 2 * cut // pl.num_programs(0)

        @pl.when(step == 0)
        def _():
            for n in range(2):
                here = slice(n * cut, (n + 1) * cut)
                side_x[here, :] = beside_all[n, :, :channels]
                side_d[here, :] = beside_all[n, :, channels : 2 * channels]
                side_m[here, :] = beside_all[n, :, 3 * channels : 3 * channels + LANES]

        beside = pl.ds(pl.multiple_of(step * each, each), each)
    x_here = pl.ds(first + step * xs, xs)
    x = state[x_here].reshape(rows, channels)
    d = pert[x_here].reshape(rows, channels)
    part = rows // chunks
    pairs = [(x[n * part : (n + 1) * part], d[n * part : (n + 1) * part]) for n in range(chunks)]
    if strips:
        h, t = pairs[-1]
        pairs[-1] = (
            jnp.concatenate([h, side_x[beside, :]], axis=0),
            jnp.concatenate([t, side_d[beside, :]], axis=0),
        )

    def at(n):
        return pl.ds(pl.multiple_of(step * rows + n * part, part), part)

    def keep(n, layer, slope):
        slopes[at(n), layer * units : (layer + 1) * units] = slope[:part].astype(BF16)

    jac = _forward(pairs, w_in, w_mid, w_out, biases, keep)

    def shift(live, value, base):
        return (base.astype(F32) + PHYS_STEP * live.astype(F32) * value).astype(BF16)

    for n in range(chunks):
        here = pl.ds(pl.multiple_of((first + step * xs) * size_y + n * part, part), part)
        base = d[n * part : (n + 1) * part, :LANES]
        moved[at(n), :] = shift(mask[here, :], jac[n][:part], base)
    if strips:
        moved_s[beside, :] = shift(side_m[beside, :], jac[-1][part:], side_d[beside, :LANES])


def forward(first, count, state, pert, mask, sides, weights):
    _, size_y, channels = state.shape
    xs = 4
    rows = xs * size_y
    layers, units = weights[3].shape
    columns = count * size_y
    args = (state, pert, mask) + sides + weights
    out = [
        jax.ShapeDtypeStruct((columns, layers * units), BF16),
        jax.ShapeDtypeStruct((columns, LANES), BF16),
    ]
    scratch = []
    if sides:
        beside = 2 * sides[0].shape[1]
        out.append(jax.ShapeDtypeStruct((beside, LANES), BF16))
        scratch = [
            pltpu.VMEM((beside, channels), BF16),
            pltpu.VMEM((beside, channels), BF16),
            pltpu.VMEM((beside, LANES), BF16),
        ]
    return pl.pallas_call(
        functools.partial(forward_kernel, first, bool(sides), rows, 2),
        grid=(count // xs,),
        in_specs=[_held()] * len(args),
        out_specs=[_held()] * len(out),
        out_shape=out,
        scratch_shapes=scratch,
        compiler_params=_params(14),
        name="forward_rest" if sides else "forward_part",
    )(*args)


def _side_picks(size_x):
    frame = size_x + 2 * REACH
    strips = REACH * size_x
    picks = np.zeros((2, frame * SIDE, LANES), np.float32)
    for x in range(size_x):
        for j in range(REACH):
            picks[0, (x + REACH) * SIDE + SIDE - REACH + j, j * size_x + x] = 1
            picks[1, (x + REACH) * SIDE + j, j * size_x + x] = 1
    for base, step, near in ((strips, -1, REACH - 1), (strips + CORNERS, 1, REACH + size_x)):
        for k, (dx, dy) in enumerate(((0, 0), (0, 1), (1, 0))):
            picks[0, (near + step * dx) * SIDE + SIDE - 1 - dy, base + k] = 1
            picks[1, (near + step * dx) * SIDE + dy, base + 3 + k] = 1
    return jnp.asarray(picks.reshape(2 * frame * SIDE, LANES), BF16)


def _place_sides(out, picks, strip_l, strip_r, ends):
    half = out.shape[0] // 2
    spare = LANES - strip_l.shape[0] - sum(e.shape[0] for e in ends)
    ends = list(ends) + [jnp.zeros((spare, out.shape[1]), BF16)]
    out[:half, :] = _dot(picks[:half, :], jnp.concatenate([strip_l] + ends, axis=0))
    out[half:, :] = _dot(picks[half:, :], jnp.concatenate([strip_r] + ends, axis=0))


def _fill(frame, own, above, below, sides, lanes, size_x, size_y, scale=None):
    row = size_y + 2 * SIDE
    count = size_x + 2 * REACH
    half = count * SIDE

    def put(at, value):
        here = slice(at, at + value.shape[0])
        frame[here, :] = value if scale is None else value * scale[here, :]

    for r in range(count):
        at = r * row
        put(at, sides[r * SIDE : (r + 1) * SIDE, lanes])
        put(at + SIDE + size_y, sides[half + r * SIDE : half + (r + 1) * SIDE, lanes])
        if r < REACH:
            value = above(slice(r * size_y, (r + 1) * size_y))
        elif r < REACH + size_x:
            value = own(r - REACH)
        else:
            k = r - REACH - size_x
            value = below(slice(k * size_y, (k + 1) * size_y))
        put(at + SIDE, value.astype(F32))


def _transport(ping, pong, kap, size_x, size_y, emit):
    row = size_y + 2 * SIDE
    count = size_x + 2 * REACH
    src, dst = ping, pong
    for step in range(1, REACH + 1):
        last = step == REACH
        start, stop = (SIDE, SIDE + size_y) if last else (0, row)
        size = (stop - start) // 2
        for lo in range(start, stop, size):
            at = step * row + lo
            prev = src[at - row : at - row + size, :]
            mid = src[at : at + size, :]
            for r in range(step, count - step):
                at = r * row + lo
                following = src[at + row : at + row + size, :]
                near = (prev + following) + (
                    src[at - 1 : at - 1 + size, :] + src[at + 1 : at + 1 + size, :]
                )
                value = mid + kap[at : at + size, :] * (near - 4.0 * mid)
                if last:
                    emit(r - REACH, lo - SIDE, size, value)
                else:
                    dst[at : at + size, :] = value
                prev, mid = mid, following
        src, dst = dst, src


def _kappa_frame(kappa, aux_l, aux_r, above, below, natural, out):
    size_x, size_y = kappa.shape
    row = size_y + 2 * SIDE
    natural[...] = jnp.zeros(natural.shape, F32)
    wide = 2 * LANES
    natural[REACH : REACH + size_x, :] = _kappa_wide(kappa, aux_l, aux_r)
    up = above[:, :wide].astype(F32) + above[:, wide : 2 * wide].astype(F32)
    down = below[:, :wide].astype(F32) + below[:, wide : 2 * wide].astype(F32)
    natural[0:REACH, :] = up[size_x - REACH :]
    natural[REACH + size_x : 2 * REACH + size_x, :] = down[:REACH]
    own = natural[:, :LANES].T
    rest = natural[:, LANES:].T
    for r in range(size_x + 2 * REACH):
        at = r * row
        put = lambda a: jnp.broadcast_to(a[:, r : r + 1], (a.shape[0], LANES))
        out[at : at + SIDE, :] = put(rest[LANES - SIDE :])
        out[at + SIDE : at + SIDE + size_y, :] = put(own)
        out[at + SIDE + size_y : at + row, :] = put(rest[:SIDE])


def _lanes(group):
    return pl.ds(pl.multiple_of(group * LANES, LANES), LANES)


def adjoint_kernel(
    adj, got_1, got_2, strips, picks, kappa, mask, slopes_a, slopes_b, w_in, w_mid, w_out,
    kap, out, ping, pong, natural, inverse, moved, sides, border,
):
    above, below = border.at[0], border.at[1]
    from_l, from_r = strips.at[0], strips.at[1]
    step = pl.program_id(0)
    groups = moved.shape[0]
    size_x, size_y = kappa.shape
    channels = adj.shape[2]
    row = size_y + 2 * SIDE
    body = REACH * size_y
    aux = 3 * channels

    @pl.when(step == 0)
    def _():
        def order(odd):
            border[0], border[1] = (got_1[...], got_2[...]) if odd else (got_2[...], got_1[...])

        _both_ways("elem", order)
        k_rows = slice(body + CORNERS, body + CORNERS + size_x)
        _kappa_frame(
            kappa, from_l[:, aux:], from_r[:, aux:], above[k_rows, :], below[k_rows, :], natural, kap
        )
        for x in range(size_x):
            at = (x + REACH) * row + SIDE
            inverse[x * size_y : (x + 1) * size_y, :] = 1.0 / kap[at : at + size_y, :]
        ends = [m[body : body + CORNERS, :channels] for m in (above, below)]
        strip = slice(2 * channels, aux)
        _place_sides(sides, picks, from_l[:, strip], from_r[:, strip], ends)

    @pl.when(step < groups)
    def _():
        lanes = _lanes(step)
        _fill(
            ping, lambda x: adj[x, :, lanes], lambda r: above[r, lanes], lambda r: below[r, lanes],
            sides, lanes, size_x, size_y, kap,
        )

        def emit(x, lo, size, value):
            here = slice(x * size_y + lo, x * size_y + lo + size)
            moved[step, here, :] = value * inverse[here, :]

        _transport(ping, pong, kap, size_x, size_y, emit)

    rows = out.shape[0]
    units = w_in.shape[1]

    def back(slopes, block, base):
        here = pl.ds(pl.multiple_of(block * rows, rows), rows)
        kept = pl.ds(pl.multiple_of((block - base) * rows, rows), rows)
        upstream = (PHYS_STEP * mask[here, :].astype(F32) * moved[0, here, :]).astype(BF16)
        half = rows // 2
        parts = [_dot_t(upstream[n * half : (n + 1) * half], w_out[...]) for n in range(2)]
        for layer in reversed(range(1 + w_mid.shape[0])):
            weights = w_in[...] if layer == 0 else w_mid[layer - 1]
            slope = slopes[kept, layer * units : (layer + 1) * units]
            for n in range(2):
                part = slope[n * half : (n + 1) * half].astype(F32)
                parts[n] = _dot_t((parts[n] * part).astype(BF16), weights)
        for n in range(2):
            at = pl.ds(pl.multiple_of(block * rows + n * half, half), half)
            for g in range(groups):
                lanes = slice(g * LANES, (g + 1) * LANES)
                out[n * half : (n + 1) * half, lanes] = moved[g, at, :] + parts[n][:, lanes]

    split = slopes_a.shape[0] // rows

    @pl.when((step >= groups) & (step < groups + split))
    def _():
        back(slopes_a, step - groups, 0)

    @pl.when(step >= groups + split)
    def _():
        back(slopes_b, step - groups, split)


def adjoint_all(adj, got, strips, kappa, mask, slopes_a, slopes_b, weights):
    size_x, size_y, channels = adj.shape
    columns = size_x * size_y
    groups = channels // LANES
    blocks = 4
    rows = columns // blocks
    frame = (size_x + 2 * REACH) * (size_y + 2 * SIDE)
    picks = _side_picks(size_x)
    args = (adj,) + got + (strips, picks, kappa, mask, slopes_a, slopes_b) + weights
    return pl.pallas_call(
        adjoint_kernel,
        grid=(groups + blocks,),
        in_specs=[_held()] * len(args),
        out_specs=[
            _held(),
            pl.BlockSpec((rows, channels), lambda i: (jnp.maximum(i - groups, 0), 0)),
        ],
        out_shape=[
            jax.ShapeDtypeStruct((frame, LANES), F32),
            jax.ShapeDtypeStruct((columns, channels), F32),
        ],
        scratch_shapes=[
            pltpu.VMEM((frame, LANES), F32),
            pltpu.VMEM((frame, LANES), F32),
            pltpu.VMEM((LANES, 2 * LANES), F32),
            pltpu.VMEM((columns, LANES), F32),
            pltpu.VMEM((groups, columns, LANES), F32),
            pltpu.VMEM((picks.shape[0], channels), F32),
            pltpu.VMEM((2,) + got[0].shape, BF16),
        ],
        compiler_params=_params(28),
        name="adjoint",
    )(*args)


def tangent_kernel(
    pert, moved_a, moved_b, late_1, late_2, strips, moved_s, picks, kap,
    out, ping, pong, sides, border,
):
    step = pl.program_id(0)
    size_x, size_y, _ = out.shape
    channels = pert.shape[2]
    cut = moved_s.shape[0] // 2
    body = REACH * size_y

    @pl.when(step == 0)
    def _():
        def order(odd):
            border[0], border[1] = (late_1[...], late_2[...]) if odd else (late_2[...], late_1[...])

        _both_ways("elem", order)
        ends = [border[n, body : body + CORNERS, :] for n in range(2)]
        beside = [
            jnp.concatenate(
                [moved_s[n * cut : (n + 1) * cut, :], strips[n, :, channels + LANES : 2 * channels]],
                axis=1,
            )
            for n in range(2)
        ]
        _place_sides(sides, picks, beside[0], beside[1], ends)

    here = _lanes(step)

    def fill(own):
        _fill(
            ping, own, lambda r: border[0, r, here], lambda r: border[1, r, here],
            sides, here, size_x, size_y,
        )

    @pl.when(step == 0)
    def _():
        split = moved_a.shape[0] // size_y

        def own(x):
            source, k = (moved_a, x) if x < split else (moved_b, x - split)
            return source[k * size_y : (k + 1) * size_y, :]

        fill(own)

    @pl.when(step > 0)
    def _():
        fill(lambda x: pert[x, :, here])

    def emit(x, lo, size, value):
        out[x, lo : lo + size, :] = value

    _transport(ping, pong, kap, size_x, size_y, emit)


def tangent_all(pert, moved_a, moved_b, late, strips, moved_s, kap):
    size_x, size_y, channels = pert.shape
    picks = _side_picks(size_x)
    args = (pert, moved_a, moved_b) + late + (strips, moved_s, picks, kap)
    return pl.pallas_call(
        tangent_kernel,
        grid=(channels // LANES,),
        in_specs=[_held()] * len(args),
        out_specs=pl.BlockSpec((size_x, size_y, LANES), lambda i: (0, 0, i)),
        out_shape=jax.ShapeDtypeStruct((size_x, size_y, channels), F32),
        scratch_shapes=[
            pltpu.VMEM(kap.shape, F32),
            pltpu.VMEM(kap.shape, F32),
            pltpu.VMEM((picks.shape[0], channels), F32),
            pltpu.VMEM((2, REACH * size_y + CORNERS, channels), BF16),
        ],
        compiler_params=_params(14),
        name="tangent",
    )(*args)


def _swap(first, second, axis):
    count = lax.axis_size(axis)
    pairs = [(i, i ^ 1) for i in range(count)]
    others = [(i, ((i + 1) ^ 1) - 1) for i in range(1, count - 1)]
    return lax.ppermute(first, axis, pairs), lax.ppermute(second, axis, others)


def per_device(
    state, perturbation, adjoint_end, kappa, act_list, counts, w_in, w_mid, w_out, biases
):
    size_x, size_y, channels = state.shape
    weights = (w_in, w_mid, w_out)
    nets = weights + (biases,)
    part = 4
    msg_1, msg_2, mask = make_edges(counts, act_list, kappa, state, perturbation, adjoint_end)
    got = _swap(msg_1, msg_2, "face")
    slopes_a, moved_a = forward(0, part, state, perturbation, mask, (), nets)
    got, slopes_a = lax.optimization_barrier((got, slopes_a))
    msg_1, msg_2, strips = first_border(kappa, got, adjoint_end)
    first = _swap(msg_1, msg_2, "elem")
    slopes_b, moved_b, moved_s = forward(
        part, size_x - part, state, perturbation, mask, (strips,), nets
    )
    late = _swap(*late_border(strips, moved_s, perturbation, moved_a, moved_b), "elem")
    kap, ad_out = adjoint_all(
        adjoint_end, first, strips, kappa, mask, slopes_a, slopes_b, weights
    )
    tl_out = tangent_all(perturbation, moved_a, moved_b, late, strips, moved_s, kap)
    return tl_out, ad_out.reshape(size_x, size_y, channels)


def solution(mesh):
    tile = P("elem", "face", None)
    plane = P("elem", "face")
    return jax.shard_map(
        per_device,
        mesh=mesh,
        in_specs=(tile, tile, tile, plane, plane, plane, P(), P(), P(), P()),
        out_specs=(tile, tile),
        check_vma=False,
    )
```

```python
import functools

import jax
import jax.numpy as jnp
import numpy as np
from jax import lax
from jax.experimental import pallas as pl
from jax.experimental.pallas import tpu as pltpu
from jax.sharding import PartitionSpec as P

PHYS_STEP = 4.0
REACH = 3
LANES = 128
SIDE = 8
CORNERS = 16
KAPPA_ROW = 8
F32 = jnp.float32
BF16 = jnp.bfloat16


def _params(mib):
    return pltpu.CompilerParams(
        dimension_semantics=("arbitrary",), vmem_limit_bytes=mib * 1024 * 1024
    )


def _held():
    return pl.BlockSpec(memory_space=pltpu.VMEM)


def _even(axis):
    return lax.axis_index(axis) % 2 == 0


def _both_ways(axis, act):
    even = _even(axis)

    @pl.when(even)
    def _():
        act(False)

    @pl.when(jnp.logical_not(even))
    def _():
        act(True)


def _dot(a, b):
    return jnp.dot(a, b, preferred_element_type=F32)


def _dot_t(a, b):
    return lax.dot_general(a, b, (((1,), (1,)), ((), ())), preferred_element_type=F32)


def _pick(shape, targets):
    row = lax.broadcasted_iota(jnp.int32, shape, 0)
    col = lax.broadcasted_iota(jnp.int32, shape, 1)
    hit = jnp.zeros(shape, jnp.bool_)
    for k, c in targets:
        hit = hit | ((row == k) & (col == c))
    return hit.astype(F32).astype(BF16)


def _split(value):
    hi = value.astype(BF16)
    return hi, (value - hi.astype(F32)).astype(BF16)


def edge_kernel(
    counts, listed_hbm, kappa_hbm, state, pert, adj, msg_1, msg_2, mask_out,
    listed, kappa, near, far, sems,
):
    size_x, size_y = kappa.shape
    width = near.shape[2]
    channels = near.shape[3]
    copies = [
        pltpu.make_async_copy(listed_hbm, listed, sems.at[0]),
        pltpu.make_async_copy(kappa_hbm, kappa, sems.at[1]),
    ]
    for n, field in enumerate((state, pert, adj)):
        low, high = pl.ds(0, width), pl.ds(size_y - width, width)
        copies.append(pltpu.make_async_copy(field.at[:, low], near.at[n], sems.at[2 + 2 * n]))
        copies.append(pltpu.make_async_copy(field.at[:, high], far.at[n], sems.at[3 + 2 * n]))
    for copy in copies:
        copy.start()
    copies[0].wait()
    copies[1].wait()
    count = counts[0, 0]
    index = listed[...]
    cap = index.shape[1]
    shift = size_y.bit_length() - 1
    pos = lax.broadcasted_iota(jnp.int32, (size_x, cap), 1)
    sub = lax.broadcasted_iota(jnp.int32, (size_x, cap), 0)
    rows = ((sub == (index >> shift)) & (pos < count)).astype(F32).astype(BF16)
    sub_y = lax.broadcasted_iota(jnp.int32, (size_y, cap), 0)
    cols = (sub_y == (index & (size_y - 1))).astype(F32).astype(BF16)
    mask = _dot_t(rows, cols)
    mask_t = _dot_t(cols, rows)
    for x in range(size_x):
        mask_out[x * size_y : (x + 1) * size_y, :] = jnp.broadcast_to(
            mask_t[:, x : x + 1], (size_y, LANES)
        ).astype(BF16)
    k_all = kappa[...]
    shape = (REACH * size_x, size_x * width)
    row = lax.broadcasted_iota(jnp.int32, shape, 0)
    col = lax.broadcasted_iota(jnp.int32, shape, 1)
    want = (row % size_x) * width + row // size_x
    for copy in copies[2:]:
        copy.wait()
    def write(left, right):
        for msg, blocks, first in ((left, near, 0), (right, far, size_y - REACH)):
            pick = (col == want + first % width).astype(F32).astype(BF16)
            for n in range(3):
                msg[:, n * channels : (n + 1) * channels] = _dot(
                    pick, blocks[n].reshape(size_x * width, channels)
                ).astype(BF16)
            at = 3 * channels
            for j in range(REACH):
                here = slice(j * size_x, (j + 1) * size_x)
                y = first + j
                hi, lo = _split(jnp.broadcast_to(k_all[:, y : y + 1], (size_x, LANES)))
                live = jnp.broadcast_to(mask[:, y : y + 1], (size_x, LANES))
                lane = lax.broadcasted_iota(jnp.int32, live.shape, 1)
                value = jnp.where(lane == 1, hi.astype(F32), live)
                value = jnp.where(lane == 2, lo.astype(F32), value)
                msg[here, at : at + LANES] = value.astype(BF16)

    _both_ways("face", lambda odd: write(msg_1, msg_2) if odd else write(msg_2, msg_1))


def make_edges(counts, listed, kappa, state, pert, adj):
    size_x, size_y, channels = state.shape
    width = 16
    strip = jax.ShapeDtypeStruct((REACH * size_x, 3 * channels + LANES), BF16)
    far = pl.BlockSpec(memory_space=pltpu.HBM)
    return pl.pallas_call(
        edge_kernel,
        in_specs=[pl.BlockSpec(memory_space=pltpu.SMEM)] + [far] * 5,
        out_specs=[_held()] * 3,
        out_shape=[strip, strip, jax.ShapeDtypeStruct((size_x * size_y, LANES), BF16)],
        scratch_shapes=[
            pltpu.VMEM(listed.shape, jnp.int32),
            pltpu.VMEM(kappa.shape, F32),
            pltpu.VMEM((3, size_x, width, channels), BF16),
            pltpu.VMEM((3, size_x, width, channels), BF16),
            pltpu.SemaphoreType.DMA((8,)),
        ],
        compiler_params=pltpu.CompilerParams(vmem_limit_bytes=12 * 1024 * 1024),
        name="edges",
    )(counts, *[pltpu.with_memory_space_constraint(a, pltpu.HBM) for a in (listed, kappa, state, pert, adj)])


def _corner_picks(size_x, top):
    near, next_ = (0, 1) if top else (size_x - 1, size_x - 2)
    left = [(0, 2 * size_x + near), (1, size_x + near), (2, 2 * size_x + next_)]
    right = [(3, near), (4, size_x + near), (5, next_)]
    shape = (CORNERS, REACH * size_x)
    return _pick(shape, left), _pick(shape, right)


def _kappa_wide(kappa, aux_l, aux_r):
    size_x, size_y = kappa.shape
    wide = jnp.concatenate([kappa[...], jnp.zeros((size_x, LANES), F32)], axis=1)
    lane = lax.broadcasted_iota(jnp.int32, wide.shape, 1)
    for aux, first in ((aux_l, wide.shape[1] - REACH), (aux_r, size_y)):
        for j in range(REACH):
            here = slice(j * size_x, (j + 1) * size_x)
            both = aux[here, :].astype(F32)
            value = jnp.broadcast_to(both[:, 1:2] + both[:, 2:3], wide.shape)
            wide = jnp.where(lane == first + j, value, wide)
    return wide


def border_kernel(kappa, got_1, got_2, adj_t, adj_b, msg_1, msg_2, strips):
    def order(odd):
        strips[0], strips[1] = (got_1[...], got_2[...]) if odd else (got_2[...], got_1[...])

    _both_ways("face", order)

    def write(odd):
        top, bot = (msg_1, msg_2) if odd else (msg_2, msg_1)
        _write_border(kappa, strips.at[0], strips.at[1], adj_t, adj_b, top, bot)

    _both_ways("elem", write)


def _write_border(kappa, from_l, from_r, adj_t, adj_b, top, bot):
    size_x, size_y = kappa.shape
    channels = adj_t.shape[2]
    body = REACH * size_y
    aux = 3 * channels
    hi, lo = _split(_kappa_wide(kappa, from_l[:, aux:], from_r[:, aux:]))
    extra = jnp.zeros((CORNERS, channels - 2 * hi.shape[1]), F32)
    for msg, adj, is_top in ((top, adj_t, True), (bot, adj_b, False)):
        first = 0 if is_top else adj.shape[0] - REACH
        msg[0:body, :] = adj[first : first + REACH].reshape(body, channels)
        pick_l, pick_r = _corner_picks(size_x, is_top)
        row = 0 if is_top else size_x - REACH
        place = _pick((CORNERS, size_x), [(KAPPA_ROW + k, row + k) for k in range(REACH)])
        here = slice(body, body + CORNERS)
        msg[here, :] = (
            _dot(pick_l, from_l[:, 2 * channels : aux])
            + _dot(pick_r, from_r[:, 2 * channels : aux])
            + jnp.concatenate([_dot(place, hi), _dot(place, lo), extra], axis=1)
        ).astype(BF16)


def first_border(kappa, got, adj):
    size_x, size_y, channels = adj.shape
    block = 4
    last = size_x // block - 1
    whole = lambda a: pl.BlockSpec(a.shape, lambda i: (0,) * a.ndim)
    low = pl.BlockSpec((block, size_y, channels), lambda i: (0, 0, 0))
    high = pl.BlockSpec((block, size_y, channels), lambda i: (last, 0, 0))
    shape = (REACH * size_y + CORNERS, channels)
    out = jax.ShapeDtypeStruct(shape, BF16)
    strips = jax.ShapeDtypeStruct((2,) + got[0].shape, BF16)
    return pl.pallas_call(
        border_kernel,
        grid=(1,),
        in_specs=[whole(kappa), whole(got[0]), whole(got[1]), low, high],
        out_specs=[whole(out), whole(out), whole(strips)],
        out_shape=[out, out, strips],
        compiler_params=_params(12),
        name="first_border",
    )(kappa, got[0], got[1], adj, adj)


def late_border_kernel(strips, moved_s, pert_t, pert_b, moved_t, moved_b, msg_1, msg_2):
    def write(odd):
        top, bot = (msg_1, msg_2) if odd else (msg_2, msg_1)
        _write_late(
            strips.at[0], strips.at[1], moved_s, pert_t, pert_b, moved_t, moved_b, top, bot
        )

    _both_ways("elem", write)


def _write_late(from_l, from_r, moved_s, pert_t, pert_b, moved_t, moved_b, top, bot):
    size_y, channels = pert_t.shape[1:]
    size_x = moved_s.shape[0] // (2 * REACH)
    body = REACH * size_y
    cut = REACH * size_x
    lanes = slice(LANES, channels)
    side = slice(channels + lanes.start, 2 * channels)
    for msg, pert, moved, is_top in (
        (top, pert_t, moved_t, True),
        (bot, pert_b, moved_b, False),
    ):
        first = 0 if is_top else pert.shape[0] - REACH
        msg[0:body, :LANES] = moved[first * size_y : (first + REACH) * size_y]
        msg[0:body, LANES:] = pert[first : first + REACH, :, lanes].reshape(
            body, channels - lanes.start
        )
        pick_l, pick_r = _corner_picks(size_x, is_top)
        msg[body:, :LANES] = (
            _dot(pick_l, moved_s[:cut]) + _dot(pick_r, moved_s[cut:])
        ).astype(BF16)
        msg[body:, LANES:] = (_dot(pick_l, from_l[:, side]) + _dot(pick_r, from_r[:, side])).astype(
            BF16
        )


def late_border(strips, moved_s, pert, moved_a, moved_b):
    size_x, size_y, channels = pert.shape
    block = 4
    last = size_x // block - 1
    end = moved_b.shape[0] // (block * size_y) - 1
    whole = lambda a: pl.BlockSpec(a.shape, lambda i: (0,) * a.ndim)
    out = jax.ShapeDtypeStruct(
        (REACH * size_y + CORNERS, channels), BF16
    )
    return pl.pallas_call(
        late_border_kernel,
        grid=(1,),
        in_specs=[
            whole(strips), whole(moved_s),
            pl.BlockSpec((block, size_y, channels), lambda i: (0, 0, 0)),
            pl.BlockSpec((block, size_y, channels), lambda i: (last, 0, 0)),
            pl.BlockSpec((block * size_y, LANES), lambda i: (0, 0)),
            pl.BlockSpec((block * size_y, LANES), lambda i: (end, 0)),
        ],
        out_specs=[whole(out)] * 2,
        out_shape=[out, out],
        compiler_params=_params(12),
        name="late_border",
    )(strips, moved_s, pert, pert, moved_a, moved_b)


def _forward(pairs, w_in, w_mid, w_out, biases, keep):
    pairs = list(pairs)
    for layer in range(1 + w_mid.shape[0]):
        weights = w_in[...] if layer == 0 else w_mid[layer - 1]
        bias = biases[layer : layer + 1, :]
        for n, (h, t) in enumerate(pairs):
            rows = h.shape[0]
            both = _dot(jnp.concatenate([h, t], axis=0), weights)
            v = jnp.tanh(both[:rows] + bias)
            slope = 1.0 - v * v
            pairs[n] = (v.astype(BF16), (slope * both[rows:]).astype(BF16))
            keep(n, layer, slope)
    return [_dot(t, w_out[...]) for _, t in pairs]


def forward_kernel(first, strips, rows, chunks, *refs):
    if strips:
        (state, pert, mask, beside_all, w_in, w_mid, w_out, biases,
         slopes, moved, moved_s, side_x, side_d, side_m) = refs
    else:
        state, pert, mask, w_in, w_mid, w_out, biases, slopes, moved = refs
    step = pl.program_id(0)
    _, size_y, channels = state.shape
    units = biases.shape[1]
    xs = rows // size_y
    if strips:
        cut = beside_all.shape[1]
        each = 2 * cut // pl.num_programs(0)

        @pl.when(step == 0)
        def _():
            for n in range(2):
                here = slice(n * cut, (n + 1) * cut)
                side_x[here, :] = beside_all[n, :, :channels]
                side_d[here, :] = beside_all[n, :, channels : 2 * channels]
                live = beside_all[n, :, 3 * channels :].astype(F32)[:, 0:1]
                side_m[here, :] = jnp.broadcast_to(live, (cut, LANES)).astype(BF16)

        beside = pl.ds(pl.multiple_of(step * each, each), each)
    x_here = pl.ds(first + step * xs, xs)
    x = state[x_here].reshape(rows, channels)
    d = pert[x_here].reshape(rows, channels)
    part = rows // chunks
    pairs = [(x[n * part : (n + 1) * part], d[n * part : (n + 1) * part]) for n in range(chunks)]
    if strips:
        h, t = pairs[-1]
        pairs[-1] = (
            jnp.concatenate([h, side_x[beside, :]], axis=0),
            jnp.concatenate([t, side_d[beside, :]], axis=0),
        )

    def at(n):
        return pl.ds(pl.multiple_of(step * rows + n * part, part), part)

    def keep(n, layer, slope):
        slopes[at(n), layer * units : (layer + 1) * units] = slope[:part].astype(BF16)

    jac = _forward(pairs, w_in, w_mid, w_out, biases, keep)

    def shift(live, value, base):
        return (base.astype(F32) + PHYS_STEP * live.astype(F32) * value).astype(BF16)

    for n in range(chunks):
        here = pl.ds(pl.multiple_of((first + step * xs) * size_y + n * part, part), part)
        base = d[n * part : (n + 1) * part, :LANES]
        moved[at(n), :] = shift(mask[here, :], jac[n][:part], base)
    if strips:
        moved_s[beside, :] = shift(side_m[beside, :], jac[-1][part:], side_d[beside, :LANES])


def forward(first, count, state, pert, mask, sides, weights):
    _, size_y, channels = state.shape
    xs = 4
    rows = xs * size_y
    layers, units = weights[3].shape
    columns = count * size_y
    args = (state, pert, mask) + sides + weights
    out = [
        jax.ShapeDtypeStruct((columns, layers * units), BF16),
        jax.ShapeDtypeStruct((columns, LANES), BF16),
    ]
    scratch = []
    if sides:
        beside = 2 * sides[0].shape[1]
        out.append(jax.ShapeDtypeStruct((beside, LANES), BF16))
        scratch = [
            pltpu.VMEM((beside, channels), BF16),
            pltpu.VMEM((beside, channels), BF16),
            pltpu.VMEM((beside, LANES), BF16),
        ]
    return pl.pallas_call(
        functools.partial(forward_kernel, first, bool(sides), rows, 2),
        grid=(count // xs,),
        in_specs=[_held()] * len(args),
        out_specs=[_held()] * len(out),
        out_shape=out,
        scratch_shapes=scratch,
        compiler_params=_params(14),
        name="forward_rest" if sides else "forward_part",
    )(*args)


def _side_picks(size_x):
    frame = size_x + 2 * REACH
    strips = REACH * size_x
    picks = np.zeros((2, frame * SIDE, LANES), np.float32)
    for x in range(size_x):
        for j in range(REACH):
            picks[0, (x + REACH) * SIDE + SIDE - REACH + j, j * size_x + x] = 1
            picks[1, (x + REACH) * SIDE + j, j * size_x + x] = 1
    for base, step, near in ((strips, -1, REACH - 1), (strips + CORNERS, 1, REACH + size_x)):
        for k, (dx, dy) in enumerate(((0, 0), (0, 1), (1, 0))):
            picks[0, (near + step * dx) * SIDE + SIDE - 1 - dy, base + k] = 1
            picks[1, (near + step * dx) * SIDE + dy, base + 3 + k] = 1
    return jnp.asarray(picks.reshape(2 * frame * SIDE, LANES), BF16)


def _place_sides(out, picks, strip_l, strip_r, ends):
    half = out.shape[0] // 2
    spare = LANES - strip_l.shape[0] - sum(e.shape[0] for e in ends)
    ends = list(ends) + [jnp.zeros((spare, out.shape[1]), BF16)]
    out[:half, :] = _dot(picks[:half, :], jnp.concatenate([strip_l] + ends, axis=0))
    out[half:, :] = _dot(picks[half:, :], jnp.concatenate([strip_r] + ends, axis=0))


def _fill(frame, own, above, below, sides, lanes, size_x, size_y, scale=None):
    row = size_y + 2 * SIDE
    count = size_x + 2 * REACH
    half = count * SIDE

    def put(at, value):
        here = slice(at, at + value.shape[0])
        frame[here, :] = value if scale is None else value * scale[here, :]

    for r in range(count):
        at = r * row
        put(at, sides[r * SIDE : (r + 1) * SIDE, lanes])
        put(at + SIDE + size_y, sides[half + r * SIDE : half + (r + 1) * SIDE, lanes])
        if r < REACH:
            value = above(slice(r * size_y, (r + 1) * size_y))
        elif r < REACH + size_x:
            value = own(r - REACH)
        else:
            k = r - REACH - size_x
            value = below(slice(k * size_y, (k + 1) * size_y))
        put(at + SIDE, value.astype(F32))


def _transport(ping, pong, kap, size_x, size_y, emit):
    row = size_y + 2 * SIDE
    count = size_x + 2 * REACH
    src, dst = ping, pong
    for step in range(1, REACH + 1):
        last = step == REACH
        start, stop = (SIDE, SIDE + size_y) if last else (0, row)
        size = (stop - start) // 2
        for lo in range(start, stop, size):
            at = step * row + lo
            prev = src[at - row : at - row + size, :]
            mid = src[at : at + size, :]
            for r in range(step, count - step):
                at = r * row + lo
                following = src[at + row : at + row + size, :]
                near = (prev + following) + (
                    src[at - 1 : at - 1 + size, :] + src[at + 1 : at + 1 + size, :]
                )
                value = mid + kap[at : at + size, :] * (near - 4.0 * mid)
                if last:
                    emit(r - REACH, lo - SIDE, size, value)
                else:
                    dst[at : at + size, :] = value
                prev, mid = mid, following
        src, dst = dst, src


def _kappa_frame(kappa, aux_l, aux_r, above, below, natural, out):
    size_x, size_y = kappa.shape
    row = size_y + 2 * SIDE
    natural[...] = jnp.zeros(natural.shape, F32)
    wide = 2 * LANES
    natural[REACH : REACH + size_x, :] = _kappa_wide(kappa, aux_l, aux_r)
    up = above[:, :wide].astype(F32) + above[:, wide : 2 * wide].astype(F32)
    down = below[:, :wide].astype(F32) + below[:, wide : 2 * wide].astype(F32)
    natural[0:REACH, :] = up[KAPPA_ROW : KAPPA_ROW + REACH]
    natural[REACH + size_x : 2 * REACH + size_x, :] = down[KAPPA_ROW : KAPPA_ROW + REACH]
    own = natural[:, :LANES].T
    rest = natural[:, LANES:].T
    for r in range(size_x + 2 * REACH):
        at = r * row
        put = lambda a: jnp.broadcast_to(a[:, r : r + 1], (a.shape[0], LANES))
        out[at : at + SIDE, :] = put(rest[LANES - SIDE :])
        out[at + SIDE : at + SIDE + size_y, :] = put(own)
        out[at + SIDE + size_y : at + row, :] = put(rest[:SIDE])


def _lanes(group):
    return pl.ds(pl.multiple_of(group * LANES, LANES), LANES)


def adjoint_kernel(
    adj, got_1, got_2, strips, picks, kappa, mask, slopes_a, slopes_b, w_in, w_mid, w_out,
    kap, out, ping, pong, natural, inverse, moved, sides, border,
):
    above, below = border.at[0], border.at[1]
    from_l, from_r = strips.at[0], strips.at[1]
    step = pl.program_id(0)
    groups = moved.shape[0]
    size_x, size_y = kappa.shape
    channels = adj.shape[2]
    row = size_y + 2 * SIDE
    body = REACH * size_y
    aux = 3 * channels

    @pl.when(step == 0)
    def _():
        def order(odd):
            border[0], border[1] = (got_1[...], got_2[...]) if odd else (got_2[...], got_1[...])

        _both_ways("elem", order)
        k_rows = slice(body, body + CORNERS)
        _kappa_frame(
            kappa, from_l[:, aux:], from_r[:, aux:], above[k_rows, :], below[k_rows, :], natural, kap
        )
        for x in range(size_x):
            at = (x + REACH) * row + SIDE
            inverse[x * size_y : (x + 1) * size_y, :] = 1.0 / kap[at : at + size_y, :]
        ends = [m[body : body + CORNERS, :channels] for m in (above, below)]
        strip = slice(2 * channels, aux)
        _place_sides(sides, picks, from_l[:, strip], from_r[:, strip], ends)

    @pl.when(step < groups)
    def _():
        lanes = _lanes(step)
        _fill(
            ping, lambda x: adj[x, :, lanes], lambda r: above[r, lanes], lambda r: below[r, lanes],
            sides, lanes, size_x, size_y, kap,
        )

        def emit(x, lo, size, value):
            here = slice(x * size_y + lo, x * size_y + lo + size)
            moved[step, here, :] = value * inverse[here, :]

        _transport(ping, pong, kap, size_x, size_y, emit)

    rows = out.shape[0]
    units = w_in.shape[1]

    def back(slopes, block, base):
        here = pl.ds(pl.multiple_of(block * rows, rows), rows)
        kept = pl.ds(pl.multiple_of((block - base) * rows, rows), rows)
        upstream = (PHYS_STEP * mask[here, :].astype(F32) * moved[0, here, :]).astype(BF16)
        half = rows // 2
        parts = [_dot_t(upstream[n * half : (n + 1) * half], w_out[...]) for n in range(2)]
        for layer in reversed(range(1 + w_mid.shape[0])):
            weights = w_in[...] if layer == 0 else w_mid[layer - 1]
            slope = slopes[kept, layer * units : (layer + 1) * units]
            for n in range(2):
                part = slope[n * half : (n + 1) * half].astype(F32)
                parts[n] = _dot_t((parts[n] * part).astype(BF16), weights)
        for n in range(2):
            at = pl.ds(pl.multiple_of(block * rows + n * half, half), half)
            for g in range(groups):
                lanes = slice(g * LANES, (g + 1) * LANES)
                out[n * half : (n + 1) * half, lanes] = moved[g, at, :] + parts[n][:, lanes]

    split = slopes_a.shape[0] // rows

    @pl.when((step >= groups) & (step < groups + split))
    def _():
        back(slopes_a, step - groups, 0)

    @pl.when(step >= groups + split)
    def _():
        back(slopes_b, step - groups, split)


def adjoint_all(adj, got, strips, kappa, mask, slopes_a, slopes_b, weights):
    size_x, size_y, channels = adj.shape
    columns = size_x * size_y
    groups = channels // LANES
    blocks = 4
    rows = columns // blocks
    frame = (size_x + 2 * REACH) * (size_y + 2 * SIDE)
    picks = _side_picks(size_x)
    args = (adj,) + got + (strips, picks, kappa, mask, slopes_a, slopes_b) + weights
    return pl.pallas_call(
        adjoint_kernel,
        grid=(groups + blocks,),
        in_specs=[_held()] * len(args),
        out_specs=[
            _held(),
            pl.BlockSpec((rows, channels), lambda i: (jnp.maximum(i - groups, 0), 0)),
        ],
        out_shape=[
            jax.ShapeDtypeStruct((frame, LANES), F32),
            jax.ShapeDtypeStruct((columns, channels), F32),
        ],
        scratch_shapes=[
            pltpu.VMEM((frame, LANES), F32),
            pltpu.VMEM((frame, LANES), F32),
            pltpu.VMEM((LANES, 2 * LANES), F32),
            pltpu.VMEM((columns, LANES), F32),
            pltpu.VMEM((groups, columns, LANES), F32),
            pltpu.VMEM((picks.shape[0], channels), F32),
            pltpu.VMEM((2,) + got[0].shape, BF16),
        ],
        compiler_params=_params(28),
        name="adjoint",
    )(*args)


def tangent_kernel(
    pert, moved_a, moved_b, late_1, late_2, strips, moved_s, picks, kap,
    out, ping, pong, sides, border,
):
    step = pl.program_id(0)
    size_x, size_y, _ = out.shape
    channels = pert.shape[2]
    cut = moved_s.shape[0] // 2
    body = REACH * size_y

    @pl.when(step == 0)
    def _():
        def order(odd):
            border[0], border[1] = (late_1[...], late_2[...]) if odd else (late_2[...], late_1[...])

        _both_ways("elem", order)
        ends = [border[n, body : body + CORNERS, :] for n in range(2)]
        beside = [
            jnp.concatenate(
                [moved_s[n * cut : (n + 1) * cut, :], strips[n, :, channels + LANES : 2 * channels]],
                axis=1,
            )
            for n in range(2)
        ]
        _place_sides(sides, picks, beside[0], beside[1], ends)

    here = _lanes(step)

    def fill(own):
        _fill(
            ping, own, lambda r: border[0, r, here], lambda r: border[1, r, here],
            sides, here, size_x, size_y,
        )

    @pl.when(step == 0)
    def _():
        split = moved_a.shape[0] // size_y

        def own(x):
            source, k = (moved_a, x) if x < split else (moved_b, x - split)
            return source[k * size_y : (k + 1) * size_y, :]

        fill(own)

    @pl.when(step > 0)
    def _():
        fill(lambda x: pert[x, :, here])

    def emit(x, lo, size, value):
        out[x, lo : lo + size, :] = value

    _transport(ping, pong, kap, size_x, size_y, emit)


def tangent_all(pert, moved_a, moved_b, late, strips, moved_s, kap):
    size_x, size_y, channels = pert.shape
    picks = _side_picks(size_x)
    args = (pert, moved_a, moved_b) + late + (strips, moved_s, picks, kap)
    return pl.pallas_call(
        tangent_kernel,
        grid=(channels // LANES,),
        in_specs=[_held()] * len(args),
        out_specs=pl.BlockSpec((size_x, size_y, LANES), lambda i: (0, 0, i)),
        out_shape=jax.ShapeDtypeStruct((size_x, size_y, channels), F32),
        scratch_shapes=[
            pltpu.VMEM(kap.shape, F32),
            pltpu.VMEM(kap.shape, F32),
            pltpu.VMEM((picks.shape[0], channels), F32),
            pltpu.VMEM((2, REACH * size_y + CORNERS, channels), BF16),
        ],
        compiler_params=_params(14),
        name="tangent",
    )(*args)


def _swap(first, second, axis):
    count = lax.axis_size(axis)
    pairs = [(i, i ^ 1) for i in range(count)]
    others = [(i, ((i + 1) ^ 1) - 1) for i in range(1, count - 1)]
    return lax.ppermute(first, axis, pairs), lax.ppermute(second, axis, others)


def per_device(
    state, perturbation, adjoint_end, kappa, act_list, counts, w_in, w_mid, w_out, biases
):
    size_x, size_y, channels = state.shape
    weights = (w_in, w_mid, w_out)
    nets = weights + (biases,)
    part = 4
    msg_1, msg_2, mask = make_edges(counts, act_list, kappa, state, perturbation, adjoint_end)
    got = _swap(msg_1, msg_2, "face")
    slopes_a, moved_a = forward(0, part, state, perturbation, mask, (), nets)
    got, slopes_a = lax.optimization_barrier((got, slopes_a))
    msg_1, msg_2, strips = first_border(kappa, got, adjoint_end)
    first = _swap(msg_1, msg_2, "elem")
    slopes_b, moved_b, moved_s = forward(
        part, size_x - part, state, perturbation, mask, (strips,), nets
    )
    late = _swap(*late_border(strips, moved_s, perturbation, moved_a, moved_b), "elem")
    kap, ad_out = adjoint_all(
        adjoint_end, first, strips, kappa, mask, slopes_a, slopes_b, weights
    )
    tl_out = tangent_all(perturbation, moved_a, moved_b, late, strips, moved_s, kap)
    return tl_out, ad_out.reshape(size_x, size_y, channels)


def solution(mesh):
    tile = P("elem", "face", None)
    plane = P("elem", "face")
    return jax.shard_map(
        per_device,
        mesh=mesh,
        in_specs=(tile, tile, tile, plane, plane, plane, P(), P(), P(), P()),
        out_specs=(tile, tile),
        check_vma=False,
    )
```

```python
import functools

import jax
import jax.numpy as jnp
import numpy as np
from jax import lax
from jax.experimental import pallas as pl
from jax.experimental.pallas import tpu as pltpu
from jax.sharding import PartitionSpec as P

PHYS_STEP = 4.0
REACH = 3
LANES = 128
SIDE = 8
CORNERS = 16
KAPPA_ROW = 8
F32 = jnp.float32
BF16 = jnp.bfloat16


def _params(mib):
    return pltpu.CompilerParams(
        dimension_semantics=("arbitrary",), vmem_limit_bytes=mib * 1024 * 1024
    )


def _held():
    return pl.BlockSpec(memory_space=pltpu.VMEM)


def _even(axis):
    return lax.axis_index(axis) % 2 == 0


def _both_ways(axis, act):
    even = _even(axis)

    @pl.when(even)
    def _():
        act(False)

    @pl.when(jnp.logical_not(even))
    def _():
        act(True)


def _dot(a, b):
    return jnp.dot(a, b, preferred_element_type=F32)


def _dot_t(a, b):
    return lax.dot_general(a, b, (((1,), (1,)), ((), ())), preferred_element_type=F32)


def _pick(shape, targets):
    row = lax.broadcasted_iota(jnp.int32, shape, 0)
    col = lax.broadcasted_iota(jnp.int32, shape, 1)
    hit = jnp.zeros(shape, jnp.bool_)
    for k, c in targets:
        hit = hit | ((row == k) & (col == c))
    return hit.astype(F32).astype(BF16)


def _split(value):
    hi = value.astype(BF16)
    return hi, (value - hi.astype(F32)).astype(BF16)


def edge_kernel(
    counts, listed_hbm, kappa_hbm, state, pert, adj, msg_1, msg_2, mask_out,
    listed, kappa, near, far, sems,
):
    size_x, size_y = kappa.shape
    width = near.shape[2]
    channels = near.shape[3]
    copies = [
        pltpu.make_async_copy(listed_hbm, listed, sems.at[0]),
        pltpu.make_async_copy(kappa_hbm, kappa, sems.at[1]),
    ]
    for n, field in enumerate((state, pert, adj)):
        low, high = pl.ds(0, width), pl.ds(size_y - width, width)
        copies.append(pltpu.make_async_copy(field.at[:, low], near.at[n], sems.at[2 + 2 * n]))
        copies.append(pltpu.make_async_copy(field.at[:, high], far.at[n], sems.at[3 + 2 * n]))
    for copy in copies:
        copy.start()
    copies[0].wait()
    copies[1].wait()
    count = counts[0, 0]
    index = listed[...]
    cap = index.shape[1]
    shift = size_y.bit_length() - 1
    pos = lax.broadcasted_iota(jnp.int32, (size_x, cap), 1)
    sub = lax.broadcasted_iota(jnp.int32, (size_x, cap), 0)
    rows = ((sub == (index >> shift)) & (pos < count)).astype(F32).astype(BF16)
    sub_y = lax.broadcasted_iota(jnp.int32, (size_y, cap), 0)
    cols = (sub_y == (index & (size_y - 1))).astype(F32).astype(BF16)
    mask = _dot_t(rows, cols)
    mask_t = _dot_t(cols, rows)
    for x in range(size_x):
        mask_out[x * size_y : (x + 1) * size_y, :] = jnp.broadcast_to(
            mask_t[:, x : x + 1], (size_y, LANES)
        ).astype(BF16)
    k_all = kappa[...]
    shape = (REACH * size_x, size_x * width)
    row = lax.broadcasted_iota(jnp.int32, shape, 0)
    col = lax.broadcasted_iota(jnp.int32, shape, 1)
    want = (row % size_x) * width + row // size_x
    for copy in copies[2:]:
        copy.wait()
    def write(left, right):
        for msg, blocks, first in ((left, near, 0), (right, far, size_y - REACH)):
            pick = (col == want + first % width).astype(F32).astype(BF16)
            for n in range(3):
                msg[:, n * channels : (n + 1) * channels] = _dot(
                    pick, blocks[n].reshape(size_x * width, channels)
                ).astype(BF16)
            at = 3 * channels
            for j in range(REACH):
                here = slice(j * size_x, (j + 1) * size_x)
                y = first + j
                hi, lo = _split(jnp.broadcast_to(k_all[:, y : y + 1], (size_x, LANES)))
                live = jnp.broadcast_to(mask[:, y : y + 1], (size_x, LANES))
                lane = lax.broadcasted_iota(jnp.int32, live.shape, 1)
                value = jnp.where(lane == 1, hi.astype(F32), live)
                value = jnp.where(lane == 2, lo.astype(F32), value)
                msg[here, at : at + LANES] = value.astype(BF16)

    _both_ways("face", lambda odd: write(msg_1, msg_2) if odd else write(msg_2, msg_1))


def make_edges(counts, listed, kappa, state, pert, adj):
    size_x, size_y, channels = state.shape
    width = 16
    strip = jax.ShapeDtypeStruct((REACH * size_x, 3 * channels + LANES), BF16)
    far = pl.BlockSpec(memory_space=pltpu.HBM)
    return pl.pallas_call(
        edge_kernel,
        in_specs=[pl.BlockSpec(memory_space=pltpu.SMEM)] + [far] * 5,
        out_specs=[_held()] * 3,
        out_shape=[strip, strip, jax.ShapeDtypeStruct((size_x * size_y, LANES), BF16)],
        scratch_shapes=[
            pltpu.VMEM(listed.shape, jnp.int32),
            pltpu.VMEM(kappa.shape, F32),
            pltpu.VMEM((3, size_x, width, channels), BF16),
            pltpu.VMEM((3, size_x, width, channels), BF16),
            pltpu.SemaphoreType.DMA((8,)),
        ],
        compiler_params=pltpu.CompilerParams(vmem_limit_bytes=12 * 1024 * 1024),
        name="edges",
    )(counts, *[pltpu.with_memory_space_constraint(a, pltpu.HBM) for a in (listed, kappa, state, pert, adj)])


def _corner_picks(size_x, top):
    near, next_ = (0, 1) if top else (size_x - 1, size_x - 2)
    left = [(0, 2 * size_x + near), (1, size_x + near), (2, 2 * size_x + next_)]
    right = [(3, near), (4, size_x + near), (5, next_)]
    shape = (CORNERS, REACH * size_x)
    return _pick(shape, left), _pick(shape, right)


def _kappa_wide(kappa, aux_l, aux_r):
    size_x, size_y = kappa.shape
    wide = jnp.concatenate([kappa[...], jnp.zeros((size_x, LANES), F32)], axis=1)
    lane = lax.broadcasted_iota(jnp.int32, wide.shape, 1)
    for aux, first in ((aux_l, wide.shape[1] - REACH), (aux_r, size_y)):
        for j in range(REACH):
            here = slice(j * size_x, (j + 1) * size_x)
            both = aux[here, :].astype(F32)
            value = jnp.broadcast_to(both[:, 1:2] + both[:, 2:3], wide.shape)
            wide = jnp.where(lane == first + j, value, wide)
    return wide


def border_kernel(kappa, got_1, got_2, adj_t, adj_b, msg_1, msg_2, strips):
    def order(odd):
        strips[0], strips[1] = (got_1[...], got_2[...]) if odd else (got_2[...], got_1[...])

    _both_ways("face", order)

    def write(odd):
        top, bot = (msg_1, msg_2) if odd else (msg_2, msg_1)
        _write_border(kappa, strips.at[0], strips.at[1], adj_t, adj_b, top, bot)

    _both_ways("elem", write)


def _write_border(kappa, from_l, from_r, adj_t, adj_b, top, bot):
    size_x, size_y = kappa.shape
    channels = adj_t.shape[2]
    body = REACH * size_y
    aux = 3 * channels
    hi, lo = _split(_kappa_wide(kappa, from_l[:, aux:], from_r[:, aux:]))
    extra = jnp.zeros((CORNERS, channels - 2 * hi.shape[1]), F32)
    for msg, adj, is_top in ((top, adj_t, True), (bot, adj_b, False)):
        first = 0 if is_top else adj.shape[0] - REACH
        msg[0:body, :] = adj[first : first + REACH].reshape(body, channels)
        pick_l, pick_r = _corner_picks(size_x, is_top)
        row = 0 if is_top else size_x - REACH
        place = _pick((CORNERS, size_x), [(KAPPA_ROW + k, row + k) for k in range(REACH)])
        here = slice(body, body + CORNERS)
        msg[here, :] = (
            _dot(pick_l, from_l[:, 2 * channels : aux])
            + _dot(pick_r, from_r[:, 2 * channels : aux])
            + jnp.concatenate([_dot(place, hi), _dot(place, lo), extra], axis=1)
        ).astype(BF16)


def first_border(kappa, got, adj):
    size_x, size_y, channels = adj.shape
    block = 4
    last = size_x // block - 1
    whole = lambda a: pl.BlockSpec(a.shape, lambda i: (0,) * a.ndim)
    low = pl.BlockSpec((block, size_y, channels), lambda i: (0, 0, 0))
    high = pl.BlockSpec((block, size_y, channels), lambda i: (last, 0, 0))
    shape = (REACH * size_y + CORNERS, channels)
    out = jax.ShapeDtypeStruct(shape, BF16)
    strips = jax.ShapeDtypeStruct((2,) + got[0].shape, BF16)
    return pl.pallas_call(
        border_kernel,
        grid=(1,),
        in_specs=[whole(kappa), whole(got[0]), whole(got[1]), low, high],
        out_specs=[whole(out), whole(out), whole(strips)],
        out_shape=[out, out, strips],
        compiler_params=_params(12),
        name="first_border",
    )(kappa, got[0], got[1], adj, adj)


def late_border_kernel(strips, moved_s, pert_t, pert_b, moved_t, moved_b, msg_1, msg_2):
    def write(odd):
        top, bot = (msg_2, msg_1) if odd else (msg_1, msg_2)
        _write_late(
            strips.at[0], strips.at[1], moved_s, pert_t, pert_b, moved_t, moved_b, top, bot
        )

    _both_ways("elem", write)


def _write_late(from_l, from_r, moved_s, pert_t, pert_b, moved_t, moved_b, top, bot):
    size_y, channels = pert_t.shape[1:]
    size_x = moved_s.shape[0] // (2 * REACH)
    body = REACH * size_y
    cut = REACH * size_x
    lanes = slice(LANES, channels)
    side = slice(channels + lanes.start, 2 * channels)
    for msg, pert, moved, is_top in (
        (top, pert_t, moved_t, True),
        (bot, pert_b, moved_b, False),
    ):
        first = 0 if is_top else pert.shape[0] - REACH
        msg[0:body, :LANES] = moved[first * size_y : (first + REACH) * size_y]
        msg[0:body, LANES:] = pert[first : first + REACH, :, lanes].reshape(
            body, channels - lanes.start
        )
        pick_l, pick_r = _corner_picks(size_x, is_top)
        msg[body:, :LANES] = (
            _dot(pick_l, moved_s[:cut]) + _dot(pick_r, moved_s[cut:])
        ).astype(BF16)
        msg[body:, LANES:] = (_dot(pick_l, from_l[:, side]) + _dot(pick_r, from_r[:, side])).astype(
            BF16
        )


def late_border(strips, moved_s, pert, moved_a, moved_b):
    size_x, size_y, channels = pert.shape
    block = 4
    last = size_x // block - 1
    end = moved_b.shape[0] // (block * size_y) - 1
    whole = lambda a: pl.BlockSpec(a.shape, lambda i: (0,) * a.ndim)
    out = jax.ShapeDtypeStruct(
        (REACH * size_y + CORNERS, channels), BF16
    )
    return pl.pallas_call(
        late_border_kernel,
        grid=(1,),
        in_specs=[
            whole(strips), whole(moved_s),
            pl.BlockSpec((block, size_y, channels), lambda i: (0, 0, 0)),
            pl.BlockSpec((block, size_y, channels), lambda i: (last, 0, 0)),
            pl.BlockSpec((block * size_y, LANES), lambda i: (0, 0)),
            pl.BlockSpec((block * size_y, LANES), lambda i: (end, 0)),
        ],
        out_specs=[whole(out)] * 2,
        out_shape=[out, out],
        compiler_params=_params(12),
        name="late_border",
    )(strips, moved_s, pert, pert, moved_a, moved_b)


def _forward(pairs, w_in, w_mid, w_out, biases, keep):
    pairs = list(pairs)
    for layer in range(1 + w_mid.shape[0]):
        weights = w_in[...] if layer == 0 else w_mid[layer - 1]
        bias = biases[layer : layer + 1, :]
        for n, (h, t) in enumerate(pairs):
            rows = h.shape[0]
            both = _dot(jnp.concatenate([h, t], axis=0), weights)
            v = jnp.tanh(both[:rows] + bias)
            slope = 1.0 - v * v
            pairs[n] = (v.astype(BF16), (slope * both[rows:]).astype(BF16))
            keep(n, layer, slope)
    return [_dot(t, w_out[...]) for _, t in pairs]


def forward_kernel(first, strips, rows, chunks, *refs):
    if strips:
        (state, pert, mask, beside_all, w_in, w_mid, w_out, biases,
         slopes, moved, moved_s, side_x, side_d, side_m) = refs
    else:
        state, pert, mask, w_in, w_mid, w_out, biases, slopes, moved = refs
    step = pl.program_id(0)
    _, size_y, channels = state.shape
    units = biases.shape[1]
    xs = rows // size_y
    if strips:
        cut = beside_all.shape[1]
        each = 2 * cut // pl.num_programs(0)

        @pl.when(step == 0)
        def _():
            for n in range(2):
                here = slice(n * cut, (n + 1) * cut)
                side_x[here, :] = beside_all[n, :, :channels]
                side_d[here, :] = beside_all[n, :, channels : 2 * channels]
                live = beside_all[n, :, 3 * channels :].astype(F32)[:, 0:1]
                side_m[here, :] = jnp.broadcast_to(live, (cut, LANES)).astype(BF16)

        beside = pl.ds(pl.multiple_of(step * each, each), each)
    x_here = pl.ds(first + step * xs, xs)
    x = state[x_here].reshape(rows, channels)
    d = pert[x_here].reshape(rows, channels)
    part = rows // chunks
    pairs = [(x[n * part : (n + 1) * part], d[n * part : (n + 1) * part]) for n in range(chunks)]
    if strips:
        h, t = pairs[-1]
        pairs[-1] = (
            jnp.concatenate([h, side_x[beside, :]], axis=0),
            jnp.concatenate([t, side_d[beside, :]], axis=0),
        )

    def at(n):
        return pl.ds(pl.multiple_of(step * rows + n * part, part), part)

    def keep(n, layer, slope):
        slopes[at(n), layer * units : (layer + 1) * units] = slope[:part].astype(BF16)

    jac = _forward(pairs, w_in, w_mid, w_out, biases, keep)

    def shift(live, value, base):
        return (base.astype(F32) + PHYS_STEP * live.astype(F32) * value).astype(BF16)

    for n in range(chunks):
        here = pl.ds(pl.multiple_of((first + step * xs) * size_y + n * part, part), part)
        base = d[n * part : (n + 1) * part, :LANES]
        moved[at(n), :] = shift(mask[here, :], jac[n][:part], base)
    if strips:
        moved_s[beside, :] = shift(side_m[beside, :], jac[-1][part:], side_d[beside, :LANES])


def forward(first, count, state, pert, mask, sides, weights):
    _, size_y, channels = state.shape
    xs = 4
    rows = xs * size_y
    layers, units = weights[3].shape
    columns = count * size_y
    args = (state, pert, mask) + sides + weights
    out = [
        jax.ShapeDtypeStruct((columns, layers * units), BF16),
        jax.ShapeDtypeStruct((columns, LANES), BF16),
    ]
    scratch = []
    if sides:
        beside = 2 * sides[0].shape[1]
        out.append(jax.ShapeDtypeStruct((beside, LANES), BF16))
        scratch = [
            pltpu.VMEM((beside, channels), BF16),
            pltpu.VMEM((beside, channels), BF16),
            pltpu.VMEM((beside, LANES), BF16),
        ]
    return pl.pallas_call(
        functools.partial(forward_kernel, first, bool(sides), rows, 2),
        grid=(count // xs,),
        in_specs=[_held()] * len(args),
        out_specs=[_held()] * len(out),
        out_shape=out,
        scratch_shapes=scratch,
        compiler_params=_params(14),
        name="forward_rest" if sides else "forward_part",
    )(*args)


def _side_picks(size_x):
    frame = size_x + 2 * REACH
    strips = REACH * size_x
    picks = np.zeros((2, frame * SIDE, LANES), np.float32)
    for x in range(size_x):
        for j in range(REACH):
            picks[0, (x + REACH) * SIDE + SIDE - REACH + j, j * size_x + x] = 1
            picks[1, (x + REACH) * SIDE + j, j * size_x + x] = 1
    for base, step, near in ((strips, -1, REACH - 1), (strips + CORNERS, 1, REACH + size_x)):
        for k, (dx, dy) in enumerate(((0, 0), (0, 1), (1, 0))):
            picks[0, (near + step * dx) * SIDE + SIDE - 1 - dy, base + k] = 1
            picks[1, (near + step * dx) * SIDE + dy, base + 3 + k] = 1
    return jnp.asarray(picks.reshape(2 * frame * SIDE, LANES), BF16)


def _place_sides(out, picks, strip_l, strip_r, ends):
    half = out.shape[0] // 2
    spare = LANES - strip_l.shape[0] - sum(e.shape[0] for e in ends)
    ends = list(ends) + [jnp.zeros((spare, out.shape[1]), BF16)]
    out[:half, :] = _dot(picks[:half, :], jnp.concatenate([strip_l] + ends, axis=0))
    out[half:, :] = _dot(picks[half:, :], jnp.concatenate([strip_r] + ends, axis=0))


def _fill(frame, own, above, below, sides, lanes, size_x, size_y, scale=None):
    row = size_y + 2 * SIDE
    count = size_x + 2 * REACH
    half = count * SIDE

    def put(at, value):
        here = slice(at, at + value.shape[0])
        frame[here, :] = value if scale is None else value * scale[here, :]

    for r in range(count):
        at = r * row
        put(at, sides[r * SIDE : (r + 1) * SIDE, lanes])
        put(at + SIDE + size_y, sides[half + r * SIDE : half + (r + 1) * SIDE, lanes])
        if r < REACH:
            value = above(slice(r * size_y, (r + 1) * size_y))
        elif r < REACH + size_x:
            value = own(r - REACH)
        else:
            k = r - REACH - size_x
            value = below(slice(k * size_y, (k + 1) * size_y))
        put(at + SIDE, value.astype(F32))


def _transport(ping, pong, kap, size_x, size_y, emit):
    row = size_y + 2 * SIDE
    count = size_x + 2 * REACH
    src, dst = ping, pong
    for step in range(1, REACH + 1):
        last = step == REACH
        start, stop = (SIDE, SIDE + size_y) if last else (0, row)
        size = (stop - start) // 2
        for lo in range(start, stop, size):
            at = step * row + lo
            prev = src[at - row : at - row + size, :]
            mid = src[at : at + size, :]
            for r in range(step, count - step):
                at = r * row + lo
                following = src[at + row : at + row + size, :]
                near = (prev + following) + (
                    src[at - 1 : at - 1 + size, :] + src[at + 1 : at + 1 + size, :]
                )
                value = mid + kap[at : at + size, :] * (near - 4.0 * mid)
                if last:
                    emit(r - REACH, lo - SIDE, size, value)
                else:
                    dst[at : at + size, :] = value
                prev, mid = mid, following
        src, dst = dst, src


def _kappa_frame(kappa, aux_l, aux_r, above, below, natural, out):
    size_x, size_y = kappa.shape
    row = size_y + 2 * SIDE
    natural[...] = jnp.zeros(natural.shape, F32)
    wide = 2 * LANES
    natural[REACH : REACH + size_x, :] = _kappa_wide(kappa, aux_l, aux_r)
    up = above[:, :wide].astype(F32) + above[:, wide : 2 * wide].astype(F32)
    down = below[:, :wide].astype(F32) + below[:, wide : 2 * wide].astype(F32)
    natural[0:REACH, :] = up[KAPPA_ROW : KAPPA_ROW + REACH]
    natural[REACH + size_x : 2 * REACH + size_x, :] = down[KAPPA_ROW : KAPPA_ROW + REACH]
    own = natural[:, :LANES].T
    rest = natural[:, LANES:].T
    for r in range(size_x + 2 * REACH):
        at = r * row
        put = lambda a: jnp.broadcast_to(a[:, r : r + 1], (a.shape[0], LANES))
        out[at : at + SIDE, :] = put(rest[LANES - SIDE :])
        out[at + SIDE : at + SIDE + size_y, :] = put(own)
        out[at + SIDE + size_y : at + row, :] = put(rest[:SIDE])


def _lanes(group):
    return pl.ds(pl.multiple_of(group * LANES, LANES), LANES)


def adjoint_kernel(
    adj, got_1, got_2, strips, picks, kappa, mask, slopes_a, slopes_b, w_in, w_mid, w_out,
    kap, out, ping, pong, natural, inverse, moved, sides, border,
):
    above, below = border.at[0], border.at[1]
    from_l, from_r = strips.at[0], strips.at[1]
    step = pl.program_id(0)
    groups = moved.shape[0]
    size_x, size_y = kappa.shape
    channels = adj.shape[2]
    row = size_y + 2 * SIDE
    body = REACH * size_y
    aux = 3 * channels

    @pl.when(step == 0)
    def _():
        def order(odd):
            border[0], border[1] = (got_1[...], got_2[...]) if odd else (got_2[...], got_1[...])

        _both_ways("elem", order)
        k_rows = slice(body, body + CORNERS)
        _kappa_frame(
            kappa, from_l[:, aux:], from_r[:, aux:], above[k_rows, :], below[k_rows, :], natural, kap
        )
        for x in range(size_x):
            at = (x + REACH) * row + SIDE
            inverse[x * size_y : (x + 1) * size_y, :] = 1.0 / kap[at : at + size_y, :]
        ends = [m[body : body + CORNERS, :channels] for m in (above, below)]
        strip = slice(2 * channels, aux)
        _place_sides(sides, picks, from_l[:, strip], from_r[:, strip], ends)

    @pl.when(step < groups)
    def _():
        lanes = _lanes(step)
        _fill(
            ping, lambda x: adj[x, :, lanes], lambda r: above[r, lanes], lambda r: below[r, lanes],
            sides, lanes, size_x, size_y, kap,
        )

        def emit(x, lo, size, value):
            here = slice(x * size_y + lo, x * size_y + lo + size)
            moved[step, here, :] = value * inverse[here, :]

        _transport(ping, pong, kap, size_x, size_y, emit)

    rows = out.shape[0]
    units = w_in.shape[1]

    def back(slopes, block, base):
        here = pl.ds(pl.multiple_of(block * rows, rows), rows)
        kept = pl.ds(pl.multiple_of((block - base) * rows, rows), rows)
        upstream = (PHYS_STEP * mask[here, :].astype(F32) * moved[0, here, :]).astype(BF16)
        half = rows // 2
        parts = [_dot_t(upstream[n * half : (n + 1) * half], w_out[...]) for n in range(2)]
        for layer in reversed(range(1 + w_mid.shape[0])):
            weights = w_in[...] if layer == 0 else w_mid[layer - 1]
            slope = slopes[kept, layer * units : (layer + 1) * units]
            for n in range(2):
                part = slope[n * half : (n + 1) * half].astype(F32)
                parts[n] = _dot_t((parts[n] * part).astype(BF16), weights)
        for n in range(2):
            at = pl.ds(pl.multiple_of(block * rows + n * half, half), half)
            for g in range(groups):
                lanes = slice(g * LANES, (g + 1) * LANES)
                out[n * half : (n + 1) * half, lanes] = moved[g, at, :] + parts[n][:, lanes]

    split = slopes_a.shape[0] // rows

    @pl.when((step >= groups) & (step < groups + split))
    def _():
        back(slopes_a, step - groups, 0)

    @pl.when(step >= groups + split)
    def _():
        back(slopes_b, step - groups, split)


def adjoint_all(adj, got, strips, kappa, mask, slopes_a, slopes_b, weights):
    size_x, size_y, channels = adj.shape
    columns = size_x * size_y
    groups = channels // LANES
    blocks = 4
    rows = columns // blocks
    frame = (size_x + 2 * REACH) * (size_y + 2 * SIDE)
    picks = _side_picks(size_x)
    args = (adj,) + got + (strips, picks, kappa, mask, slopes_a, slopes_b) + weights
    return pl.pallas_call(
        adjoint_kernel,
        grid=(groups + blocks,),
        in_specs=[_held()] * len(args),
        out_specs=[
            _held(),
            pl.BlockSpec((rows, channels), lambda i: (jnp.maximum(i - groups, 0), 0)),
        ],
        out_shape=[
            jax.ShapeDtypeStruct((frame, LANES), F32),
            jax.ShapeDtypeStruct((columns, channels), F32),
        ],
        scratch_shapes=[
            pltpu.VMEM((frame, LANES), F32),
            pltpu.VMEM((frame, LANES), F32),
            pltpu.VMEM((LANES, 2 * LANES), F32),
            pltpu.VMEM((columns, LANES), F32),
            pltpu.VMEM((groups, columns, LANES), F32),
            pltpu.VMEM((picks.shape[0], channels), F32),
            pltpu.VMEM((2,) + got[0].shape, BF16),
        ],
        compiler_params=_params(28),
        name="adjoint",
    )(*args)


def tangent_kernel(
    pert, moved_a, moved_b, late_1, late_2, strips, moved_s, picks, kap,
    out, ping, pong, sides, border,
):
    step = pl.program_id(0)
    size_x, size_y, _ = out.shape
    channels = pert.shape[2]
    cut = moved_s.shape[0] // 2
    body = REACH * size_y

    @pl.when(step == 0)
    def _():
        def order(odd):
            border[0], border[1] = (late_2[...], late_1[...]) if odd else (late_1[...], late_2[...])

        _both_ways("elem", order)
        ends = [border[n, body : body + CORNERS, :] for n in range(2)]
        beside = [
            jnp.concatenate(
                [moved_s[n * cut : (n + 1) * cut, :], strips[n, :, channels + LANES : 2 * channels]],
                axis=1,
            )
            for n in range(2)
        ]
        _place_sides(sides, picks, beside[0], beside[1], ends)

    here = _lanes(step)

    def fill(own):
        _fill(
            ping, own, lambda r: border[0, r, here], lambda r: border[1, r, here],
            sides, here, size_x, size_y,
        )

    @pl.when(step == 0)
    def _():
        split = moved_a.shape[0] // size_y

        def own(x):
            source, k = (moved_a, x) if x < split else (moved_b, x - split)
            return source[k * size_y : (k + 1) * size_y, :]

        fill(own)

    @pl.when(step > 0)
    def _():
        fill(lambda x: pert[x, :, here])

    def emit(x, lo, size, value):
        out[x, lo : lo + size, :] = value

    _transport(ping, pong, kap, size_x, size_y, emit)


def tangent_all(pert, moved_a, moved_b, late, strips, moved_s, kap):
    size_x, size_y, channels = pert.shape
    picks = _side_picks(size_x)
    args = (pert, moved_a, moved_b) + late + (strips, moved_s, picks, kap)
    return pl.pallas_call(
        tangent_kernel,
        grid=(channels // LANES,),
        in_specs=[_held()] * len(args),
        out_specs=pl.BlockSpec((size_x, size_y, LANES), lambda i: (0, 0, i)),
        out_shape=jax.ShapeDtypeStruct((size_x, size_y, channels), F32),
        scratch_shapes=[
            pltpu.VMEM(kap.shape, F32),
            pltpu.VMEM(kap.shape, F32),
            pltpu.VMEM((picks.shape[0], channels), F32),
            pltpu.VMEM((2, REACH * size_y + CORNERS, channels), BF16),
        ],
        compiler_params=_params(14),
        name="tangent",
    )(*args)


def _swap(first, second, axis, flip=False):
    count = lax.axis_size(axis)
    pairs = [(i, i ^ 1) for i in range(count)]
    others = [(i, ((i + 1) ^ 1) - 1) for i in range(1, count - 1)]
    if flip:
        pairs, others = others, pairs
    return lax.ppermute(first, axis, pairs), lax.ppermute(second, axis, others)


def per_device(
    state, perturbation, adjoint_end, kappa, act_list, counts, w_in, w_mid, w_out, biases
):
    size_x, size_y, channels = state.shape
    weights = (w_in, w_mid, w_out)
    nets = weights + (biases,)
    part = 4
    msg_1, msg_2, mask = make_edges(counts, act_list, kappa, state, perturbation, adjoint_end)
    got = _swap(msg_1, msg_2, "face")
    slopes_a, moved_a = forward(0, part, state, perturbation, mask, (), nets)
    got, slopes_a = lax.optimization_barrier((got, slopes_a))
    msg_1, msg_2, strips = first_border(kappa, got, adjoint_end)
    first = _swap(msg_1, msg_2, "elem")
    slopes_b, moved_b, moved_s = forward(
        part, size_x - part, state, perturbation, mask, (strips,), nets
    )
    late = _swap(*late_border(strips, moved_s, perturbation, moved_a, moved_b), "elem", True)
    kap, ad_out = adjoint_all(
        adjoint_end, first, strips, kappa, mask, slopes_a, slopes_b, weights
    )
    tl_out = tangent_all(perturbation, moved_a, moved_b, late, strips, moved_s, kap)
    return tl_out, ad_out.reshape(size_x, size_y, channels)


def solution(mesh):
    tile = P("elem", "face", None)
    plane = P("elem", "face")
    return jax.shard_map(
        per_device,
        mesh=mesh,
        in_specs=(tile, tile, tile, plane, plane, plane, P(), P(), P(), P()),
        out_specs=(tile, tile),
        check_vma=False,
    )
```
